128 devices in a mesh: trow: 16 (over y, z), tcol: 8 (over x, core).
Axes of the slice: x: 4, y: 4, z: 4, core: 2. Of those that a mesh axis runs over, the one named last changes fastest.
Arguments:
- mask_level: float32 [16384, 16384], P('trow', 'tcol'), may hold values from -8 to 8
- target: bfloat16 [16384, 16384], P('trow', 'tcol'), may hold values from 0 to 1
- kernels: float32 [12, 2, 128, 128], replicated, may hold values from -2.2888184e-05 to 2.2888184e-05
- step_sizes: float32 [3], replicated, may hold values from 0.25 to 2
- density_class: int32 [32, 32], P('trow', 'tcol'), may hold values from 0 to 3, as said below
- work_list: int32 [128], replicated, may hold values from 0 to 1023, as said below
Outputs:
- mask_level_new: float32 [16384, 16384], P('trow', 'tcol')
The draws below stay inside these ranges and needn't reach their ends.
Inputs may be any that keep to these rules, and one draw needn't show every extreme that they name: `density_class`: exactly 128 tiles are busy (class 1 to 3); the others are empty (class 0). The 2 x 4 tiles held by one device (tile rows 2 r, 2 r + 1 and tile columns 4 c .. 4 c + 3) hold at most 4 busy tiles, and some device's tiles hold exactly 4. `work_list`: entry d is the number a * 32 + b of the busy tile that device d computes, devices counted with trow slowest; its entries are distinct and are exactly the busy tiles.
All inputs are finite; a program needn't handle non-finite values.
Results may differ from the reference program's by a relative error of at most 0.005.
Values may be sent and summed in bfloat16 or wider, within the bound.
A program may use at most 128 MiB of HBM per device.

```python
import math
import jax
import jax.numpy as jnp
from jax import lax

TILE = 512
APRON = 64
FREQ = 128
KERNELS = 12
LEVELS = 3
MOST = 4
PAD = 640
TILE_ROWS = 32
TILE_COLS = 32
TILES = 1024
WORKERS = 128
NX = 16384
NY = 16384


def busy_order(key):
    count = TILE_ROWS * TILE_COLS
    blocks = count // 8
    numbers = jnp.arange(count, dtype=jnp.int32)
    tile_row = numbers // TILE_COLS
    tile_col = numbers % TILE_COLS
    block = tile_row // 2 * (TILE_COLS // 4) + tile_col // 4
    local = tile_row % 2 * 4 + tile_col % 4
    local_keys = jax.random.randint(jax.random.fold_in(key, 11), (count,), 0, 1 << 20).astype(jnp.int32)
    table = jnp.zeros((count,), jnp.int32).at[block * 8 + local].set(local_keys).reshape(blocks, 8)
    places = jnp.arange(8, dtype=jnp.int32)
    before = (table[:, None, :] < table[:, :, None]) | (table[:, None, :] == table[:, :, None]) & (places[None, None, :] < places[None, :, None])
    ranks = jnp.sum(before.astype(jnp.int32), 2).reshape(count)
    eligible = ranks[block * 8 + local] < MOST
    heat = jax.random.randint(jax.random.fold_in(key, 12), (blocks,), 0, 4).astype(jnp.int32)[block]
    base = jax.random.randint(jax.random.fold_in(key, 13), (count,), 0, 3 << 20).astype(jnp.int32) - heat * (1 << 20)
    chosen = jax.random.randint(jax.random.fold_in(key, 14), (), 0, blocks).astype(jnp.int32)
    scores = jnp.where(eligible, jnp.where(block == chosen, -(1 << 28), base), 1 << 29)
    return jnp.argsort(scores, stable=True).astype(jnp.int32)


def draw_density_class(key, part):
    order = busy_order(key)
    key = jax.random.fold_in(key, 3)
    count = TILE_ROWS * TILE_COLS
    levels = jax.random.randint(key, (count,), 1, LEVELS + 1).astype(jnp.int32)
    busy = jnp.zeros((count,), jnp.int32).at[order[:WORKERS]].set(1)
    return (busy * levels).reshape(TILE_ROWS, TILE_COLS)


def draw_work_list(key, part):
    order = busy_order(key)
    key = jax.random.fold_in(key, 4)
    shuffle = jax.random.permutation(key, WORKERS)
    return order[:WORKERS][shuffle].astype(jnp.int32)


def level_of(key, extent, shards, low, largest):
    level, own = 1.0, jax.random.fold_in(key, 6)
    for dim, parts in shards:
        heights = jnp.exp(jax.random.uniform(jax.random.fold_in(own, dim), (parts,), jnp.float32, low / len(shards), largest / len(shards)))
        level = level * jnp.repeat(heights, extent[dim] // parts).reshape([-1 if axis == dim else 1 for axis in range(len(extent))])
    return level


def noise(rng, shape, width, most, cuts=(), held_as=jnp.bfloat16):
    loudness = level_of(rng, shape, cuts, -0.22, 0.18) if cuts else 1.0
    entries = jax.random.normal(rng, shape, jnp.float32) * width * loudness
    return jnp.minimum(jnp.maximum(entries, -most), most).astype(held_as)


def setup_inputs(seed: int = 0) -> dict:
    key_list = jax.random.split(jax.random.key(seed), 7)
    return {
        "mask_level": noise(key_list[0], (NX, NY), 2.0, 8.0, ((0, 16), (1, 8)), jnp.float32),
        "target": jnp.clip(1.0 * jax.random.uniform(key_list[1], (NX, NY), jnp.float32) ** level_of(key_list[1], (NX, NY), ((0, 16), (1, 8)), -0.2, 0.2), 0.0, 1.0).astype(jnp.bfloat16),
        "kernels": noise(key_list[2], (KERNELS, 2, FREQ, FREQ), (PAD * PAD * FREQ * FREQ * KERNELS * 4 // 5) ** -0.5, 2.288818359375e-05, (), jnp.float32),
        "step_sizes": jnp.clip(jnp.exp(jax.random.uniform(key_list[3], (LEVELS,), jnp.float32, math.log(0.25), math.log(2.0))), 0.25, 2.0),
        "density_class": draw_density_class(jax.random.fold_in(key_list[6], 71), 0),
        "work_list": draw_work_list(jax.random.fold_in(key_list[6], 71), 0),
    }


RESIST_SLOPE = 4.0
RESIST_LEVEL = 1.0


def spectral_tables(pad_side, tile_side, freq_count):
    freq_index = jnp.arange(freq_count, dtype=jnp.int32) - freq_count // 2
    positions = jnp.arange(pad_side, dtype=jnp.int32)
    turns = (freq_index[:, None] * positions[None, :]) % pad_side
    angles = turns.astype(jnp.float32) * (2.0 * math.pi / pad_side)
    cosines = jnp.cos(angles).astype(jnp.bfloat16)
    sines = jnp.sin(angles).astype(jnp.bfloat16)
    margin = (pad_side - tile_side) // 2
    return cosines, sines, cosines[:, margin:margin + tile_side], sines[:, margin:margin + tile_side]


def tile_gradient(extended, target_tile, kernels):
    pad_side = extended.shape[0]
    tile_side = target_tile.shape[0]
    freq_count = kernels.shape[-1]
    cosines, sines, core_cos, core_sin = spectral_tables(pad_side, tile_side, freq_count)
    full_rows = jnp.concatenate([cosines, sines], 0)
    row_spectra = jnp.dot(full_rows, extended, preferred_element_type=jnp.float32).astype(jnp.bfloat16)
    blocks = jnp.dot(row_spectra, full_rows.T, preferred_element_type=jnp.float32)
    spec_re = blocks[:freq_count, :freq_count] - blocks[freq_count:, freq_count:]
    spec_im = -(blocks[:freq_count, freq_count:] + blocks[freq_count:, :freq_count])
    inverse_right = jnp.concatenate([core_cos, core_sin], 1)
    inverse_rows = jnp.concatenate([core_cos, core_sin], 0)
    inverse_left = inverse_rows.T

    def half_inverse(part_re, part_im):
        stacked = jnp.concatenate([part_re, part_im], 0)
        product = jnp.dot(stacked, inverse_right, preferred_element_type=jnp.float32)
        out_re = product[:freq_count, :tile_side] - product[freq_count:, tile_side:]
        out_im = product[:freq_count, tile_side:] + product[freq_count:, :tile_side]
        return out_re.astype(jnp.bfloat16), out_im.astype(jnp.bfloat16)

    def forward_kernel(carry, kernel):
        kern_re = kernel[0]
        kern_im = kernel[1]
        spec_z_re = (kern_re * spec_re - kern_im * spec_im).astype(jnp.bfloat16)
        spec_z_im = (kern_re * spec_im + kern_im * spec_re).astype(jnp.bfloat16)
        half_re, half_im = half_inverse(spec_z_re, spec_z_im)
        block = jnp.concatenate([jnp.concatenate([half_re, half_im], 1), jnp.concatenate([-half_im, half_re], 1)], 0)
        field = jnp.dot(inverse_left, block, preferred_element_type=jnp.float32).astype(jnp.bfloat16)
        squares = field.astype(jnp.float32) ** 2
        return carry + squares[:, :tile_side] + squares[:, tile_side:], field

    intensity, fields = lax.scan(forward_kernel, jnp.zeros((tile_side, tile_side), jnp.float32), kernels)
    resist = jax.nn.sigmoid(RESIST_SLOPE * (intensity - RESIST_LEVEL))
    weight = 2.0 * (resist - target_tile.astype(jnp.float32)) * RESIST_SLOPE * resist * (1.0 - resist)
    doubled = jnp.concatenate([2.0 * weight, 2.0 * weight], 1)

    def adjoint_kernel(carry, pair):
        kernel, field = pair
        kern_re = kernel[0]
        kern_im = kernel[1]
        pulled = (doubled * field.astype(jnp.float32)).astype(jnp.bfloat16)
        middle = jnp.dot(inverse_rows, pulled, preferred_element_type=jnp.float32)
        back_re = (middle[:freq_count, :tile_side] + middle[freq_count:, tile_side:]).astype(jnp.bfloat16)
        back_im = (middle[:freq_count, tile_side:] - middle[freq_count:, :tile_side]).astype(jnp.bfloat16)
        spectral = jnp.dot(jnp.concatenate([back_re, back_im], 0), inverse_left, preferred_element_type=jnp.float32)
        grad_re = spectral[:freq_count, :freq_count] + spectral[freq_count:, freq_count:]
        grad_im = spectral[freq_count:, :freq_count] - spectral[:freq_count, freq_count:]
        total_re = carry[0] + kern_re * grad_re + kern_im * grad_im
        total_im = carry[1] + kern_re * grad_im - kern_im * grad_re
        return (total_re, total_im), None

    empty = jnp.zeros((freq_count, freq_count), jnp.float32)
    totals, unused = lax.scan(adjoint_kernel, (empty, empty), (kernels, fields))
    last_re, last_im = half_inverse(totals[0].astype(jnp.bfloat16), totals[1].astype(jnp.bfloat16))
    return jnp.dot(inverse_left, jnp.concatenate([last_re, -last_im], 0), preferred_element_type=jnp.float32)


def reference(mask_level, target, kernels, step_sizes, density_class, work_list):
    squashed = jax.nn.sigmoid(mask_level)
    trans = (2.0 * squashed - 1.0).astype(jnp.bfloat16)
    padded = jnp.pad(trans, APRON)

    def one_tile(tile_number):
        tile_row = (tile_number // TILE_COLS).astype(jnp.int32)
        tile_col = (tile_number % TILE_COLS).astype(jnp.int32)
        start_row = (tile_row * TILE).astype(jnp.int32)
        start_col = (tile_col * TILE).astype(jnp.int32)
        extended = lax.dynamic_slice(padded, (start_row, start_col), (PAD, PAD))
        target_tile = lax.dynamic_slice(target, (start_row, start_col), (TILE, TILE))
        return tile_gradient(extended, target_tile, kernels)

    grads = lax.map(one_tile, work_list)
    per_tile = jnp.zeros((TILES, TILE, TILE), jnp.float32).at[work_list].set(grads)
    grid = per_tile.reshape(TILE_ROWS, TILE_COLS, TILE, TILE).transpose(0, 2, 1, 3)
    level_match = (density_class[:, :, None] == jnp.arange(1, LEVELS + 1, dtype=jnp.int32)[None, None, :]).astype(jnp.float32)
    tile_steps = jnp.sum(level_match * step_sizes[None, None, :], 2)
    scaled = (tile_steps[:, None, :, None] * grid).reshape(NX, NY)
    return mask_level - scaled * (2.0 * squashed * (1.0 - squashed))
```

```python
import functools

import jax
import jax.numpy as jnp
import ml_dtypes
import numpy as np
from jax import lax
from jax.experimental import pallas as pl
from jax.experimental.pallas import tpu as pltpu
from jax.sharding import PartitionSpec as P

TILE = 512
APRON = 64
PAD = TILE + 2 * APRON
FREQ = 128
KERNELS = 12
MOST = 4
SLOTS = 8
COLS = 4
GRID = 256
SIDE = 128
WIDE = TILE + 2 * SIDE
ROWS_HERE = 2 * TILE
COLS_HERE = COLS * TILE
BF = jnp.bfloat16
F32 = jnp.float32


def tables():
    freq = np.arange(FREQ, dtype=np.int64) - FREQ // 2

    def waves(count, period):
        turns = (freq[:, None] * np.arange(count)[None, :]) % period
        angles = turns * (2.0 * np.pi / period)
        return np.cos(angles), np.sin(angles)

    cos, sin = waves(PAD, PAD)
    spread = np.zeros((WIDE, 2 * FREQ))
    spread[SIDE - APRON : SIDE + TILE + APRON] = np.concatenate([cos, sin], 0).T
    rows = np.concatenate([cos, sin], 0)
    cg, sg = waves(GRID, GRID)
    coarse = np.block([[cg, sg], [-sg, cg]])
    core_cos, core_sin = cos[:, APRON : APRON + TILE], sin[:, APRON : APRON + TILE]
    fine = np.block([[core_cos, core_sin], [-core_sin, core_cos]])
    back = np.concatenate([core_cos, -core_sin], 0).T
    gap = np.arange(APRON, APRON + TILE)[:, None] - np.arange(GRID)[None, :] * (PAD / GRID)
    degree = np.arange(1, FREQ)
    lift = 1.0 + 2.0 * np.cos(gap[:, :, None] * degree * (2.0 * np.pi / PAD)).sum(2)
    lift = lift / GRID
    return [
        np.ascontiguousarray(t).astype(ml_dtypes.bfloat16)
        for t in (spread, rows, coarse, coarse.T, lift, lift.T, fine, back)
    ]


TABLE_SHAPES = (
    (WIDE, 2 * FREQ),
    (2 * FREQ, PAD),
    (2 * FREQ, 2 * GRID),
    (2 * GRID, 2 * FREQ),
    (TILE, GRID),
    (GRID, TILE),
    (2 * FREQ, 2 * TILE),
    (TILE, 2 * FREQ),
)


def dot(a, b):
    return jnp.dot(a, b, preferred_element_type=F32)


def step_kernel(
    cls_ref,
    steps_ref,
    mask_hbm,
    target_hbm,
    wide_hbm,
    kern_hbm,
    *rest,
):
    n_tab = len(TABLE_SHAPES)
    tab_hbm, rest = rest[:n_tab], rest[n_tab:]
    out_hbm = rest[0]
    (
        slot_ref,
        kern,
        ext,
        goal,
        mask,
        result,
        zbuf,
        wbuf,
        field,
        inten,
        tab_sem,
        kern_sem,
        ext_sem,
        goal_sem,
        mask_sem,
        out_sem,
        keep_sem,
        *tabs,
    ) = rest[1:]
    spread, rows, coarse, coarse_t, lift, lift_t, fine, back = tabs

    count = jnp.int32(0)
    for s in range(SLOTS):
        busy = cls_ref[s // COLS, s % COLS] > 0

        @pl.when(busy)
        def _(s=s, count=count):
            slot_ref[count] = s

        count = count + busy.astype(jnp.int32)

    def corner(s):
        r, c = s // COLS, s % COLS
        return pl.multiple_of(r * TILE, TILE), pl.multiple_of(c * TILE, TILE)

    def ext_copy(i):
        r, c = corner(slot_ref[i])
        return pltpu.make_async_copy(
            wide_hbm.at[pl.ds(r, PAD), pl.ds(c, WIDE)], ext.at[i], ext_sem.at[i]
        )

    def goal_copy(i):
        r, c = corner(slot_ref[i])
        return pltpu.make_async_copy(
            target_hbm.at[pl.ds(r, TILE), pl.ds(c, TILE)], goal.at[i], goal_sem.at[i]
        )

    def mask_copy(i):
        r, c = corner(slot_ref[i])
        return pltpu.make_async_copy(
            mask_hbm.at[pl.ds(r, TILE), pl.ds(c, TILE)], mask.at[i], mask_sem.at[i]
        )

    def out_copy(i):
        r, c = corner(slot_ref[i])
        return pltpu.make_async_copy(
            result.at[i], out_hbm.at[pl.ds(r, TILE), pl.ds(c, TILE)], out_sem.at[i]
        )

    def keep_copy(s):
        r, c = (s // COLS) * TILE, (s % COLS) * TILE
        return pltpu.make_async_copy(
            mask_hbm.at[pl.ds(r, TILE), pl.ds(c, TILE)],
            out_hbm.at[pl.ds(r, TILE), pl.ds(c, TILE)],
            keep_sem.at[s],
        )

    def tab_copy(t):
        return pltpu.make_async_copy(tab_hbm[t], tabs[t], tab_sem.at[t])

    kern_copy = pltpu.make_async_copy(kern_hbm, kern, kern_sem)

    tab_copy(0).start()

    @pl.when(count > 0)
    def _():
        ext_copy(0).start()

    tab_copy(1).start()
    kern_copy.start()
    for t in range(2, n_tab):
        tab_copy(t).start()

    @pl.when(count > 0)
    def _():
        goal_copy(0).start()
        mask_copy(0).start()

    def fetch(i, _):
        ext_copy(i).start()
        goal_copy(i).start()
        mask_copy(i).start()
        return 0

    lax.fori_loop(1, count, fetch, 0)
    for s in range(SLOTS):

        @pl.when(cls_ref[s // COLS, s % COLS] <= 0)
        def _(s=s):
            keep_copy(s).start()

    for t in range(n_tab):
        tab_copy(t).wait()
    kern_copy.wait()

    def tile(i, _):
        ext_copy(i).wait()
        first = dot(ext[i], spread[...]).astype(BF)
        blocks = dot(rows[...], first)
        spec_re = blocks[:FREQ, :FREQ] - blocks[FREQ:, FREQ:]
        spec_im = -(blocks[:FREQ, FREQ:] + blocks[FREQ:, :FREQ])

        for k in range(KERNELS):
            h_re, h_im = kern[k, 0], kern[k, 1]
            z_re = (h_re * spec_re - h_im * spec_im).astype(BF)
            z_im = (h_re * spec_im + h_im * spec_re).astype(BF)
            w = dot(jnp.concatenate([z_re, z_im], 1), coarse[...]).astype(BF)
            f = dot(coarse_t[...], jnp.concatenate([w[:, :GRID], w[:, GRID:]], 0))
            field[k] = f.astype(BF)
            square = f[:GRID] * f[:GRID] + f[GRID:] * f[GRID:]
            if k == 0:
                inten[...] = square - 1.0
            else:
                inten[...] += square

        goal_copy(i).wait()
        half = dot(lift[...], inten[...].astype(BF)).astype(BF)
        above = dot(half, lift_t[...])
        resist = 0.5 + 0.5 * jnp.tanh(2.0 * above)
        weight = (8.0 * (resist - goal[i].astype(F32))) * (resist * (1.0 - resist))
        drop = dot(lift_t[...], weight.astype(BF)).astype(BF)
        pull = (2.0 * dot(drop, lift[...])).astype(BF)

        tot_re = jnp.zeros((FREQ, FREQ), F32)
        tot_im = jnp.zeros((FREQ, FREQ), F32)
        for k in range(KERNELS):
            pulled = field[k] * jnp.concatenate([pull, pull], 0)
            y = dot(coarse[...], pulled).astype(BF)
            g = dot(jnp.concatenate([y[:FREQ], y[FREQ:]], 1), coarse_t[...])
            g_re, g_im = g[:, :FREQ], g[:, FREQ:]
            h_re, h_im = kern[k, 0], kern[k, 1]
            tot_re = tot_re + h_re * g_re + h_im * g_im
            tot_im = tot_im + h_re * g_im - h_im * g_re

        v = dot(jnp.concatenate([tot_re, tot_im], 1).astype(BF), fine[...]).astype(BF)
        grad = dot(back[...], jnp.concatenate([v[:, :TILE], v[:, TILE:]], 0))
        slot = slot_ref[i]
        level = cls_ref[slot // COLS, slot % COLS]
        size = 0.5 * steps_ref[level - 1]
        mask_copy(i).wait()
        here = mask[i]
        trans = jnp.tanh(0.5 * here)
        result[i] = here - (size * grad) * (1.0 - trans * trans)
        out_copy(i).start()
        return 0

    lax.fori_loop(0, count, tile, 0)

    def drain(i, _):
        out_copy(i).wait()
        return 0

    lax.fori_loop(0, count, drain, 0)
    for s in range(SLOTS):

        @pl.when(cls_ref[s // COLS, s % COLS] <= 0)
        def _(s=s):
            keep_copy(s).wait()


def take_step(cls, steps, mask, target, wide, kernels, tabs):
    any_spec = pl.BlockSpec(memory_space=pl.ANY)
    smem = pl.BlockSpec(memory_space=pltpu.SMEM)
    dma = pltpu.SemaphoreType.DMA
    return pl.pallas_call(
        step_kernel,
        out_shape=jax.ShapeDtypeStruct((ROWS_HERE, COLS_HERE), F32),
        in_specs=[smem, smem] + [any_spec] * (4 + len(TABLE_SHAPES)),
        out_specs=any_spec,
        scratch_shapes=[
            pltpu.SMEM((SLOTS,), jnp.int32),
            pltpu.VMEM((KERNELS, 2, FREQ, FREQ), F32),
            pltpu.VMEM((MOST, PAD, WIDE), BF),
            pltpu.VMEM((MOST, TILE, TILE), BF),
            pltpu.VMEM((MOST, TILE, TILE), F32),
            pltpu.VMEM((MOST, TILE, TILE), F32),
            pltpu.VMEM((KERNELS, FREQ, 2 * FREQ), BF),
            pltpu.VMEM((KERNELS, 2 * FREQ, GRID), BF),
            pltpu.VMEM((KERNELS, 2 * GRID, GRID), BF),
            pltpu.VMEM((GRID, GRID), F32),
            dma((len(TABLE_SHAPES),)),
            dma,
            dma((MOST,)),
            dma((MOST,)),
            dma((MOST,)),
            dma((MOST,)),
            dma((SLOTS,)),
        ]
        + [pltpu.VMEM(s, BF) for s in TABLE_SHAPES],
        compiler_params=pltpu.CompilerParams(vmem_limit_bytes=56 * 1024 * 1024),
        cost_estimate=pl.CostEstimate(
            flops=30_000_000_000, bytes_accessed=40_000_000, transcendentals=3_000_000
        ),
    )(cls, steps, mask, target, wide, kernels, *tabs)


CORNERS = ((-1, -1), (-1, 1), (1, -1), (1, 1))
SIDES = ((-1, 0), (1, 0), (0, -1), (0, 1)) + CORNERS
CHUNK = 128
CHUNKS = ROWS_HERE // CHUNK


def margin_kernel(
    n_rows,
    n_cols,
    mask_hbm,
    wide_hbm,
    rows_in,
    cols_in,
    rows_out,
    cols_out,
    corners_out,
    chunk_in,
    chunk_out,
    in_sem,
    chunk_sem,
    store_sem,
    send_sem,
    recv_sem,
):
    row, col = lax.axis_index("trow"), lax.axis_index("tcol")

    def near(dr, dc):
        return (lax.rem(row + dr + n_rows, n_rows), lax.rem(col + dc + n_cols, n_cols))

    barrier = pltpu.get_barrier_semaphore()
    for dr, dc in SIDES:
        pl.semaphore_signal(
            barrier, inc=1, device_id=near(dr, dc), device_id_type=pl.DeviceIdType.MESH
        )

    strips = []
    for side in range(2):
        start = side * (ROWS_HERE - APRON)
        strips.append(
            pltpu.make_async_copy(
                mask_hbm.at[pl.ds(start, APRON), :], rows_in.at[side], in_sem.at[side]
            )
        )
        start = side * (COLS_HERE - SIDE)
        strips.append(
            pltpu.make_async_copy(
                mask_hbm.at[:, pl.ds(start, SIDE)], cols_in.at[side], in_sem.at[2 + side]
            )
        )
    for copy in strips:
        copy.start()

    def load(n):
        return pltpu.make_async_copy(
            mask_hbm.at[pl.ds(n * CHUNK, CHUNK), :], chunk_in.at[n % 3], chunk_sem.at[n % 3]
        )

    def store(n):
        return pltpu.make_async_copy(
            chunk_out.at[n % 2],
            wide_hbm.at[pl.ds(APRON + n * CHUNK, CHUNK), pl.ds(SIDE, COLS_HERE)],
            store_sem.at[n % 2],
        )

    load(0).start()
    load(1).start()

    inside_r = [(row > 0).astype(F32), (row < n_rows - 1).astype(F32)]
    inside_c = [(col > 0).astype(F32), (col < n_cols - 1).astype(F32)]
    for copy in strips:
        copy.wait()
    for side in range(2):
        strip = jnp.tanh(0.5 * rows_in[side]) * inside_r[side]
        rows_out[side] = strip.astype(BF)
        for other in range(2):
            cut = strip[:, :SIDE] if other == 0 else strip[:, COLS_HERE - SIDE :]
            corners_out[2 * side + other] = (cut * inside_c[other]).astype(BF)
        cols_out[side] = (jnp.tanh(0.5 * cols_in[side]) * inside_c[side]).astype(BF)

    pl.semaphore_wait(barrier, len(SIDES))

    row_place = {-1: pl.ds(APRON + ROWS_HERE, APRON), 1: pl.ds(0, APRON), 0: pl.ds(APRON, ROWS_HERE)}
    col_place = {-1: pl.ds(SIDE + COLS_HERE, SIDE), 1: pl.ds(0, SIDE), 0: pl.ds(SIDE, COLS_HERE)}
    sources = [
        rows_out.at[0],
        rows_out.at[1],
        cols_out.at[0],
        cols_out.at[1],
    ] + [corners_out.at[n] for n in range(4)]
    sends = []
    for n, (dr, dc) in enumerate(SIDES):
        sends.append(
            pltpu.make_async_remote_copy(
                src_ref=sources[n],
                dst_ref=wide_hbm.at[row_place[dr], col_place[dc]],
                send_sem=send_sem.at[n],
                recv_sem=recv_sem.at[n],
                device_id=near(dr, dc),
                device_id_type=pl.DeviceIdType.MESH,
            )
        )
    for send in sends:
        send.start()

    for n in range(CHUNKS):
        if n + 2 < CHUNKS:
            load(n + 2).start()
        load(n).wait()
        if n >= 2:
            store(n - 2).wait()
        chunk_out[n % 2] = jnp.tanh(0.5 * chunk_in[n % 3]).astype(BF)
        store(n).start()
    store(CHUNKS - 2).wait()
    store(CHUNKS - 1).wait()
    for send in sends:
        send.wait()


def widen(mask, n_rows, n_cols):
    any_spec = pl.BlockSpec(memory_space=pl.ANY)
    dma = pltpu.SemaphoreType.DMA
    return pl.pallas_call(
        functools.partial(margin_kernel, n_rows, n_cols),
        out_shape=jax.ShapeDtypeStruct((ROWS_HERE + 2 * APRON, COLS_HERE + 2 * SIDE), BF),
        in_specs=[any_spec],
        out_specs=any_spec,
        scratch_shapes=[
            pltpu.VMEM((2, APRON, COLS_HERE), F32),
            pltpu.VMEM((2, ROWS_HERE, SIDE), F32),
            pltpu.VMEM((2, APRON, COLS_HERE), BF),
            pltpu.VMEM((2, ROWS_HERE, SIDE), BF),
            pltpu.VMEM((4, APRON, SIDE), BF),
            pltpu.VMEM((3, CHUNK, COLS_HERE), F32),
            pltpu.VMEM((2, CHUNK, COLS_HERE), BF),
            dma((4,)),
            dma((3,)),
            dma((2,)),
            dma((len(SIDES),)),
            dma((len(SIDES),)),
        ],
        compiler_params=pltpu.CompilerParams(
            collective_id=0, has_side_effects=True, vmem_limit_bytes=32 * 1024 * 1024
        ),
        cost_estimate=pl.CostEstimate(
            flops=10_000_000, bytes_accessed=14_000_000, transcendentals=2_000_000
        ),
    )(mask)


def body(mask_level, target, kernels, step_sizes, density_class, work_list):
    wide = widen(mask_level, lax.axis_size("trow"), lax.axis_size("tcol"))
    tabs = [jnp.asarray(t) for t in tables()]
    return take_step(density_class, step_sizes, mask_level, target, wide, kernels, tabs)


def solution(mesh):
    return jax.shard_map(
        body,
        mesh=mesh,
        in_specs=(P("trow", "tcol"), P("trow", "tcol"), P(), P(), P("trow", "tcol"), P()),
        out_specs=P("trow", "tcol"),
        check_vma=False,
    )
```

```python
import functools

import jax
import jax.numpy as jnp
import ml_dtypes
import numpy as np
from jax import lax
from jax.experimental import pallas as pl
from jax.experimental.pallas import tpu as pltpu
from jax.sharding import PartitionSpec as P

TILE = 512
APRON = 64
PAD = TILE + 2 * APRON
FREQ = 128
KERNELS = 12
MOST = 4
SLOTS = 8
COLS = 4
GRID = 256
SIDE = 128
WIDE = TILE + 2 * SIDE
ROWS_HERE = 2 * TILE
COLS_HERE = COLS * TILE
BF = jnp.bfloat16
F32 = jnp.float32


def tables():
    freq = np.arange(FREQ, dtype=np.int64) - FREQ // 2

    def waves(count, period):
        turns = (freq[:, None] * np.arange(count)[None, :]) % period
        angles = turns * (2.0 * np.pi / period)
        return np.cos(angles), np.sin(angles)

    cos, sin = waves(PAD, PAD)
    spread = np.zeros((WIDE, 2 * FREQ))
    spread[SIDE - APRON : SIDE + TILE + APRON] = np.concatenate([cos, sin], 0).T
    rows = np.concatenate([cos, sin], 0)
    cg, sg = waves(GRID, GRID)
    coarse = np.block([[cg, sg], [-sg, cg]])
    core_cos, core_sin = cos[:, APRON : APRON + TILE], sin[:, APRON : APRON + TILE]
    fine = np.block([[core_cos, core_sin], [-core_sin, core_cos]])
    back = np.concatenate([core_cos, -core_sin], 0).T
    gap = np.arange(APRON, APRON + TILE)[:, None] - np.arange(GRID)[None, :] * (PAD / GRID)
    degree = np.arange(1, FREQ)
    lift = 1.0 + 2.0 * np.cos(gap[:, :, None] * degree * (2.0 * np.pi / PAD)).sum(2)
    lift = lift / GRID
    return [
        np.ascontiguousarray(t).astype(ml_dtypes.bfloat16)
        for t in (spread, rows, coarse, coarse.T, lift, lift.T, fine, back)
    ]


TABLE_SHAPES = (
    (WIDE, 2 * FREQ),
    (2 * FREQ, PAD),
    (2 * FREQ, 2 * GRID),
    (2 * GRID, 2 * FREQ),
    (TILE, GRID),
    (GRID, TILE),
    (2 * FREQ, 2 * TILE),
    (TILE, 2 * FREQ),
)


def dot(a, b):
    return jnp.dot(a, b, preferred_element_type=F32)


def step_kernel(
    cls_ref,
    steps_ref,
    mask_hbm,
    target_hbm,
    wide,
    kern,
    spread,
    rows,
    coarse,
    coarse_t,
    lift,
    lift_t,
    fine,
    back,
    out_hbm,
    slot_ref,
    goal,
    mask,
    field,
    inten,
    goal_sem,
    mask_sem,
    out_sem,
):
    count = jnp.int32(0)
    for s in range(SLOTS):
        busy = cls_ref[s // COLS, s % COLS] > 0

        @pl.when(busy)
        def _(s=s, count=count):
            slot_ref[count] = s

        count = count + busy.astype(jnp.int32)

    def corner(s):
        r, c = s // COLS, s % COLS
        return pl.multiple_of(r * TILE, TILE), pl.multiple_of(c * TILE, TILE)

    def goal_copy(i):
        r, c = corner(slot_ref[i])
        return pltpu.make_async_copy(
            target_hbm.at[pl.ds(r, TILE), pl.ds(c, TILE)], goal.at[i], goal_sem.at[i]
        )

    def mask_copy(s):
        r, c = (s // COLS) * TILE, (s % COLS) * TILE
        return pltpu.make_async_copy(
            mask_hbm.at[pl.ds(r, TILE), pl.ds(c, TILE)], mask.at[s], mask_sem.at[s]
        )

    def out_copy(s):
        r, c = corner(s)
        return pltpu.make_async_copy(
            mask.at[s], out_hbm.at[pl.ds(r, TILE), pl.ds(c, TILE)], out_sem.at[s]
        )

    def fetch(i, _):
        goal_copy(i).start()
        return 0

    lax.fori_loop(0, count, fetch, 0)
    for s in range(SLOTS):
        mask_copy(s).start()
    for s in range(SLOTS):
        mask_copy(s).wait()

        @pl.when(cls_ref[s // COLS, s % COLS] <= 0)
        def _(s=s):
            out_copy(s).start()

    def tile(i, _):
        slot = slot_ref[i]
        r, c = corner(slot)
        first = dot(wide[pl.ds(r, PAD), pl.ds(c, WIDE)], spread[...]).astype(BF)
        blocks = dot(rows[...], first)
        spec_re = blocks[:FREQ, :FREQ] - blocks[FREQ:, FREQ:]
        spec_im = -(blocks[:FREQ, FREQ:] + blocks[FREQ:, :FREQ])

        for k in range(KERNELS):
            h_re, h_im = kern[k, 0], kern[k, 1]
            z_re = (h_re * spec_re - h_im * spec_im).astype(BF)
            z_im = (h_re * spec_im + h_im * spec_re).astype(BF)
            w = dot(jnp.concatenate([z_re, z_im], 1), coarse[...]).astype(BF)
            f = dot(coarse_t[...], jnp.concatenate([w[:, :GRID], w[:, GRID:]], 0))
            field[k] = f.astype(BF)
            square = f[:GRID] * f[:GRID] + f[GRID:] * f[GRID:]
            if k == 0:
                inten[...] = square - 1.0
            else:
                inten[...] += square

        goal_copy(i).wait()
        half = dot(lift[...], inten[...].astype(BF)).astype(BF)
        above = dot(half, lift_t[...])
        resist = 0.5 + 0.5 * jnp.tanh(2.0 * above)
        weight = (8.0 * (resist - goal[i].astype(F32))) * (resist * (1.0 - resist))
        drop = dot(lift_t[...], weight.astype(BF)).astype(BF)
        pull = (2.0 * dot(drop, lift[...])).astype(BF)

        tot_re = jnp.zeros((FREQ, FREQ), F32)
        tot_im = jnp.zeros((FREQ, FREQ), F32)
        for k in range(KERNELS):
            pulled = field[k] * jnp.concatenate([pull, pull], 0)
            y = dot(coarse[...], pulled).astype(BF)
            g = dot(jnp.concatenate([y[:FREQ], y[FREQ:]], 1), coarse_t[...])
            g_re, g_im = g[:, :FREQ], g[:, FREQ:]
            h_re, h_im = kern[k, 0], kern[k, 1]
            tot_re = tot_re + h_re * g_re + h_im * g_im
            tot_im = tot_im + h_re * g_im - h_im * g_re

        v = dot(jnp.concatenate([tot_re, tot_im], 1).astype(BF), fine[...]).astype(BF)
        grad = dot(back[...], jnp.concatenate([v[:, :TILE], v[:, TILE:]], 0))
        level = cls_ref[slot // COLS, slot % COLS]
        size = 0.5 * steps_ref[level - 1]
        here = mask[slot]
        trans = jnp.tanh(0.5 * here)
        mask[slot] = here - (size * grad) * (1.0 - trans * trans)
        out_copy(slot).start()
        return 0

    lax.fori_loop(0, count, tile, 0)

    for s in range(SLOTS):
        out_copy(s).wait()


def take_step(cls, steps, mask, target, wide, kernels, tabs):
    hbm = pl.BlockSpec(memory_space=pltpu.HBM)
    vmem = pl.BlockSpec(memory_space=pltpu.VMEM)
    smem = pl.BlockSpec(memory_space=pltpu.SMEM)
    dma = pltpu.SemaphoreType.DMA
    here = pltpu.with_memory_space_constraint
    return pl.pallas_call(
        step_kernel,
        out_shape=jax.ShapeDtypeStruct((ROWS_HERE, COLS_HERE), F32),
        in_specs=[smem, smem, hbm, hbm, vmem, vmem] + [vmem] * len(TABLE_SHAPES),
        out_specs=hbm,
        scratch_shapes=[
            pltpu.SMEM((SLOTS,), jnp.int32),
            pltpu.VMEM((MOST, TILE, TILE), BF),
            pltpu.VMEM((SLOTS, TILE, TILE), F32),
            pltpu.VMEM((KERNELS, 2 * GRID, GRID), BF),
            pltpu.VMEM((GRID, GRID), F32),
            dma((MOST,)),
            dma((SLOTS,)),
            dma((SLOTS,)),
        ],
        compiler_params=pltpu.CompilerParams(vmem_limit_bytes=32 * 1024 * 1024),
        cost_estimate=pl.CostEstimate(
            flops=30_000_000_000, bytes_accessed=40_000_000, transcendentals=3_000_000
        ),
    )(
        cls,
        steps,
        here(mask, pltpu.HBM),
        here(target, pltpu.HBM),
        here(wide, pltpu.VMEM),
        here(kernels, pltpu.VMEM),
        *[here(t, pltpu.VMEM) for t in tabs],
    )


CORNERS = ((-1, -1), (-1, 1), (1, -1), (1, 1))
SIDES = ((-1, 0), (1, 0), (0, -1), (0, 1)) + CORNERS
CHUNK = 128
CHUNKS = ROWS_HERE // CHUNK


def margin_kernel(
    n_rows,
    n_cols,
    mask_hbm,
    wide,
    rows_in,
    cols_in,
    rows_out,
    cols_out,
    corners_out,
    chunk_in,
    chunk_out,
    in_sem,
    chunk_sem,
    store_sem,
    send_sem,
    recv_sem,
):
    row, col = lax.axis_index("trow"), lax.axis_index("tcol")

    def near(dr, dc):
        return (lax.rem(row + dr + n_rows, n_rows), lax.rem(col + dc + n_cols, n_cols))

    barrier = pltpu.get_barrier_semaphore()
    for dr, dc in SIDES:
        pl.semaphore_signal(
            barrier, inc=1, device_id=near(dr, dc), device_id_type=pl.DeviceIdType.MESH
        )

    strips = []
    for side in range(2):
        start = side * (ROWS_HERE - APRON)
        strips.append(
            pltpu.make_async_copy(
                mask_hbm.at[pl.ds(start, APRON), :], rows_in.at[side], in_sem.at[side]
            )
        )
        start = side * (COLS_HERE - SIDE)
        strips.append(
            pltpu.make_async_copy(
                mask_hbm.at[:, pl.ds(start, SIDE)], cols_in.at[side], in_sem.at[2 + side]
            )
        )
    for copy in strips:
        copy.start()

    def load(n):
        return pltpu.make_async_copy(
            mask_hbm.at[pl.ds(n * CHUNK, CHUNK), :], chunk_in.at[n % 3], chunk_sem.at[n % 3]
        )

    def store(n):
        return pltpu.make_async_copy(
            chunk_out.at[n % 2],
            wide.at[pl.ds(APRON + n * CHUNK, CHUNK), pl.ds(SIDE, COLS_HERE)],
            store_sem.at[n % 2],
        )

    load(0).start()
    load(1).start()

    inside_r = [(row > 0).astype(F32), (row < n_rows - 1).astype(F32)]
    inside_c = [(col > 0).astype(F32), (col < n_cols - 1).astype(F32)]
    for copy in strips:
        copy.wait()
    for side in range(2):
        strip = jnp.tanh(0.5 * rows_in[side]) * inside_r[side]
        rows_out[side] = strip.astype(BF)
        for other in range(2):
            cut = strip[:, :SIDE] if other == 0 else strip[:, COLS_HERE - SIDE :]
            corners_out[2 * side + other] = (cut * inside_c[other]).astype(BF)
        cols_out[side] = (jnp.tanh(0.5 * cols_in[side]) * inside_c[side]).astype(BF)

    pl.semaphore_wait(barrier, len(SIDES))

    row_place = {-1: pl.ds(APRON + ROWS_HERE, APRON), 1: pl.ds(0, APRON), 0: pl.ds(APRON, ROWS_HERE)}
    col_place = {-1: pl.ds(SIDE + COLS_HERE, SIDE), 1: pl.ds(0, SIDE), 0: pl.ds(SIDE, COLS_HERE)}
    sources = [
        rows_out.at[0],
        rows_out.at[1],
        cols_out.at[0],
        cols_out.at[1],
    ] + [corners_out.at[n] for n in range(4)]
    sends = []
    for n, (dr, dc) in enumerate(SIDES):
        sends.append(
            pltpu.make_async_remote_copy(
                src_ref=sources[n],
                dst_ref=wide.at[row_place[dr], col_place[dc]],
                send_sem=send_sem.at[n],
                recv_sem=recv_sem.at[n],
                device_id=near(dr, dc),
                device_id_type=pl.DeviceIdType.MESH,
            )
        )
    for send in sends:
        send.start()

    for n in range(CHUNKS):
        if n + 2 < CHUNKS:
            load(n + 2).start()
        load(n).wait()
        if n >= 2:
            store(n - 2).wait()
        chunk_out[n % 2] = jnp.tanh(0.5 * chunk_in[n % 3]).astype(BF)
        store(n).start()
    store(CHUNKS - 2).wait()
    store(CHUNKS - 1).wait()
    for send in sends:
        send.wait()


def widen(mask, n_rows, n_cols):
    dma = pltpu.SemaphoreType.DMA
    return pl.pallas_call(
        functools.partial(margin_kernel, n_rows, n_cols),
        out_shape=pltpu.VMEM((ROWS_HERE + 2 * APRON, COLS_HERE + 2 * SIDE), BF),
        in_specs=[pl.BlockSpec(memory_space=pltpu.HBM)],
        out_specs=pl.BlockSpec(memory_space=pltpu.VMEM),
        scratch_shapes=[
            pltpu.VMEM((2, APRON, COLS_HERE), F32),
            pltpu.VMEM((2, ROWS_HERE, SIDE), F32),
            pltpu.VMEM((2, APRON, COLS_HERE), BF),
            pltpu.VMEM((2, ROWS_HERE, SIDE), BF),
            pltpu.VMEM((4, APRON, SIDE), BF),
            pltpu.VMEM((3, CHUNK, COLS_HERE), F32),
            pltpu.VMEM((2, CHUNK, COLS_HERE), BF),
            dma((4,)),
            dma((3,)),
            dma((2,)),
            dma((len(SIDES),)),
            dma((len(SIDES),)),
        ],
        compiler_params=pltpu.CompilerParams(
            collective_id=0, has_side_effects=True, vmem_limit_bytes=32 * 1024 * 1024
        ),
        cost_estimate=pl.CostEstimate(
            flops=10_000_000, bytes_accessed=14_000_000, transcendentals=2_000_000
        ),
    )(pltpu.with_memory_space_constraint(mask, pltpu.HBM))


def body(mask_level, target, kernels, step_sizes, density_class, work_list):
    wide = widen(mask_level, lax.axis_size("trow"), lax.axis_size("tcol"))
    tabs = [jnp.asarray(t) for t in tables()]
    return take_step(density_class, step_sizes, mask_level, target, wide, kernels, tabs)


def solution(mesh):
    return jax.shard_map(
        body,
        mesh=mesh,
        in_specs=(P("trow", "tcol"), P("trow", "tcol"), P(), P(), P("trow", "tcol"), P()),
        out_specs=P("trow", "tcol"),
        check_vma=False,
    )
```

```python
import functools

import jax
import jax.numpy as jnp
import ml_dtypes
import numpy as np
from jax import lax
from jax.experimental import pallas as pl
from jax.experimental.pallas import tpu as pltpu
from jax.sharding import PartitionSpec as P

TILE = 512
APRON = 64
PAD = TILE + 2 * APRON
FREQ = 128
KERNELS = 12
MOST = 4
SLOTS = 8
GROUP = 12
LANES = 2
COLS = 4
GRID = 256
SIDE = 128
WIDE = TILE + 2 * SIDE
ROWS_HERE = 2 * TILE
COLS_HERE = COLS * TILE
BF = jnp.bfloat16
F32 = jnp.float32


def tables():
    freq = np.arange(FREQ, dtype=np.int64) - FREQ // 2

    def waves(count, period):
        turns = (freq[:, None] * np.arange(count)[None, :]) % period
        angles = turns * (2.0 * np.pi / period)
        return np.cos(angles), np.sin(angles)

    cos, sin = waves(PAD, PAD)
    spread = np.zeros((WIDE, 2 * FREQ))
    spread[SIDE - APRON : SIDE + TILE + APRON] = np.concatenate([cos, sin], 0).T
    rows = np.concatenate([cos, sin], 0)
    cg, sg = waves(GRID, GRID)
    coarse = np.block([[cg, sg], [-sg, cg]])
    core_cos, core_sin = cos[:, APRON : APRON + TILE], sin[:, APRON : APRON + TILE]
    fine = np.block([[core_cos, core_sin], [-core_sin, core_cos]])
    back = np.concatenate([core_cos, -core_sin], 0).T
    gap = np.arange(APRON, APRON + TILE)[:, None] - np.arange(GRID)[None, :] * (PAD / GRID)
    degree = np.arange(1, FREQ)
    lift = 1.0 + 2.0 * np.cos(gap[:, :, None] * degree * (2.0 * np.pi / PAD)).sum(2)
    lift = lift / GRID
    return [
        np.ascontiguousarray(t).astype(ml_dtypes.bfloat16)
        for t in (spread, rows, coarse, coarse.T, lift, lift.T, fine, back)
    ]


TABLE_SHAPES = (
    (WIDE, 2 * FREQ),
    (2 * FREQ, PAD),
    (2 * FREQ, 2 * GRID),
    (2 * GRID, 2 * FREQ),
    (TILE, GRID),
    (GRID, TILE),
    (2 * FREQ, 2 * TILE),
    (TILE, 2 * FREQ),
)


def dot(a, b):
    return jnp.dot(a, b, preferred_element_type=F32)


def step_kernel(
    cls_ref,
    steps_ref,
    mask_hbm,
    target_hbm,
    wide,
    kern,
    spread,
    rows,
    coarse,
    coarse_t,
    lift,
    lift_t,
    fine,
    back,
    out_hbm,
    slot_ref,
    goal,
    mask,
    result,
    field,
    inten,
    goal_sem,
    mask_sem,
    out_sem,
    keep_sem,
):
    count = jnp.int32(0)
    for s in range(SLOTS):
        busy = cls_ref[s // COLS, s % COLS] > 0

        @pl.when(busy)
        def _(s=s, count=count):
            slot_ref[count] = s

        count = count + busy.astype(jnp.int32)

    def corner(s):
        r, c = s // COLS, s % COLS
        return pl.multiple_of(r * TILE, TILE), pl.multiple_of(c * TILE, TILE)

    def goal_copy(i):
        r, c = corner(slot_ref[i])
        return pltpu.make_async_copy(
            target_hbm.at[pl.ds(r, TILE), pl.ds(c, TILE)], goal.at[i], goal_sem.at[i]
        )

    def mask_copy(s):
        r, c = (s // COLS) * TILE, (s % COLS) * TILE
        return pltpu.make_async_copy(
            mask_hbm.at[pl.ds(r, TILE), pl.ds(c, TILE)], mask.at[s], mask_sem.at[s]
        )

    def keep_copy(s):
        r, c = (s // COLS) * TILE, (s % COLS) * TILE
        return pltpu.make_async_copy(
            mask.at[s], out_hbm.at[pl.ds(r, TILE), pl.ds(c, TILE)], keep_sem.at[s]
        )

    def out_copy(i):
        r, c = corner(slot_ref[i])
        return pltpu.make_async_copy(
            result.at[i], out_hbm.at[pl.ds(r, TILE), pl.ds(c, TILE)], out_sem.at[i]
        )

    def fetch(i, _):
        goal_copy(i).start()
        return 0

    lax.fori_loop(0, count, fetch, 0)
    for s in range(SLOTS):
        mask_copy(s).start()

    def keep():
        for s in range(SLOTS):
            mask_copy(s).wait()

            @pl.when(cls_ref[s // COLS, s % COLS] <= 0)
            def _(s=s):
                keep_copy(s).start()

    @pl.when(count == 0)
    def _():
        keep()

    def spectrum(t):
        first = dot(wide[pl.ds(t.r, PAD), pl.ds(t.c, WIDE)], spread[...]).astype(BF)
        blocks = dot(rows[...], first)
        re = blocks[:FREQ, :FREQ] - blocks[FREQ:, FREQ:]
        im = -(blocks[:FREQ, FREQ:] + blocks[FREQ:, :FREQ])
        t.spec_re = jnp.concatenate([re, re], 1)
        t.spec_im = jnp.concatenate([im, im], 1)

    def forward(t, k):
        parts = []
        for p in range(k, k + GROUP, 2):
            h_re = jnp.concatenate([kern[p, 0], kern[p + 1, 0]], 1)
            h_im = jnp.concatenate([kern[p, 1], kern[p + 1, 1]], 1)
            z_re = (h_re * t.spec_re - h_im * t.spec_im).astype(BF)
            z_im = (h_re * t.spec_im + h_im * t.spec_re).astype(BF)
            w = dot(coarse_t[...], jnp.concatenate([z_re, z_im], 0)).astype(BF)
            for n in range(2):
                cut = w[:, n * FREQ : (n + 1) * FREQ]
                parts.append(jnp.concatenate([cut[:GRID], cut[GRID:]], 1))
        f = dot(jnp.concatenate(parts, 0), coarse[...])
        total = None
        for n in range(GROUP):
            one = f[n * GRID : (n + 1) * GRID]
            field[t.lane, k + n] = one.astype(BF)
            square = one[:, :GRID] * one[:, :GRID] + one[:, GRID:] * one[:, GRID:]
            total = square if total is None else total + square
        if k == 0:
            inten[t.lane] = total - 1.0
        else:
            inten[t.lane] += total

    def resist(t):
        half = dot(lift[...], (2.0 * inten[t.lane]).astype(BF)).astype(BF)
        bend = jnp.tanh(dot(half, lift_t[...]))
        weight = (1.0 + bend - 2.0 * goal[t.i].astype(F32)) * (1.0 - bend * bend)
        drop = dot(lift_t[...], weight.astype(BF)).astype(BF)
        pull = (2.0 * dot(drop, lift[...])).astype(BF)
        t.pull = jnp.concatenate([pull, pull], 1)
        t.tot_re = jnp.zeros((FREQ, 2 * FREQ), F32)
        t.tot_im = jnp.zeros((FREQ, 2 * FREQ), F32)

    def adjoint(t, k):
        pulled = jnp.concatenate([field[t.lane, k + n] * t.pull for n in range(GROUP)], 0)
        x = dot(pulled, coarse_t[...]).astype(BF)
        for p in range(0, GROUP, 2):
            a = x[p * GRID : (p + 1) * GRID]
            b = x[(p + 1) * GRID : (p + 2) * GRID]
            pair = jnp.concatenate(
                [
                    jnp.concatenate([a[:, :FREQ], b[:, :FREQ]], 1),
                    jnp.concatenate([a[:, FREQ:], b[:, FREQ:]], 1),
                ],
                0,
            )
            g = dot(coarse[...], pair)
            g_re, g_im = g[:FREQ], g[FREQ:]
            h_re = jnp.concatenate([kern[k + p, 0], kern[k + p + 1, 0]], 1)
            h_im = jnp.concatenate([kern[k + p, 1], kern[k + p + 1, 1]], 1)
            t.tot_re = t.tot_re + h_re * g_re + h_im * g_im
            t.tot_im = t.tot_im + h_re * g_im - h_im * g_re

    def finish(t):
        level = cls_ref[t.slot // COLS, t.slot % COLS]
        size = 0.5 * steps_ref[level - 1]
        tot_re = size * (t.tot_re[:, :FREQ] + t.tot_re[:, FREQ:])
        tot_im = size * (t.tot_im[:, :FREQ] + t.tot_im[:, FREQ:])
        v = dot(jnp.concatenate([tot_re, tot_im], 1).astype(BF), fine[...]).astype(BF)
        grad = dot(back[...], jnp.concatenate([v[:, :TILE], v[:, TILE:]], 0))
        here = mask[t.slot]
        trans = jnp.tanh(0.5 * here)
        result[t.i] = here - grad * (1.0 - trans * trans)

    class Tile:
        def __init__(self, i, lane):
            self.i, self.lane = i, lane
            self.slot = slot_ref[i]
            self.r, self.c = corner(self.slot)

    def batch(b, _):
        start = b * LANES
        tiles = [Tile(jnp.minimum(start + n, count - 1), n) for n in range(LANES)]
        for t in tiles:
            spectrum(t)
        for k in range(0, KERNELS, GROUP):
            for t in tiles:
                forward(t, k)

        @pl.when(b == 0)
        def _():
            keep()
            lax.fori_loop(0, count, lambda i, _: (goal_copy(i).wait(), 0)[1], 0)

        for t in tiles:
            resist(t)
        for k in range(0, KERNELS, GROUP):
            for t in tiles:
                adjoint(t, k)
        for t in tiles:
            finish(t)
        for n in range(LANES):

            @pl.when(start + n < count)
            def _(n=n):
                out_copy(start + n).start()

        return 0

    lax.fori_loop(0, (count + LANES - 1) // LANES, batch, 0)

    lax.fori_loop(0, count, lambda i, _: (out_copy(i).wait(), 0)[1], 0)
    for s in range(SLOTS):

        @pl.when(cls_ref[s // COLS, s % COLS] <= 0)
        def _(s=s):
            keep_copy(s).wait()


def take_step(cls, steps, mask, target, wide, kernels, tabs):
    hbm = pl.BlockSpec(memory_space=pltpu.HBM)
    vmem = pl.BlockSpec(memory_space=pltpu.VMEM)
    smem = pl.BlockSpec(memory_space=pltpu.SMEM)
    dma = pltpu.SemaphoreType.DMA
    here = pltpu.with_memory_space_constraint
    return pl.pallas_call(
        step_kernel,
        out_shape=jax.ShapeDtypeStruct((ROWS_HERE, COLS_HERE), F32),
        in_specs=[smem, smem, hbm, hbm, vmem, vmem] + [vmem] * len(TABLE_SHAPES),
        out_specs=hbm,
        scratch_shapes=[
            pltpu.SMEM((SLOTS,), jnp.int32),
            pltpu.VMEM((MOST, TILE, TILE), BF),
            pltpu.VMEM((SLOTS, TILE, TILE), F32),
            pltpu.VMEM((MOST, TILE, TILE), F32),
            pltpu.VMEM((LANES, KERNELS, GRID, 2 * GRID), BF),
            pltpu.VMEM((LANES, GRID, GRID), F32),
            dma((MOST,)),
            dma((SLOTS,)),
            dma((MOST,)),
            dma((SLOTS,)),
        ],
        compiler_params=pltpu.CompilerParams(vmem_limit_bytes=48 * 1024 * 1024),
        cost_estimate=pl.CostEstimate(
            flops=30_000_000_000, bytes_accessed=40_000_000, transcendentals=3_000_000
        ),
    )(
        cls,
        steps,
        here(mask, pltpu.HBM),
        here(target, pltpu.HBM),
        here(wide, pltpu.VMEM),
        here(kernels, pltpu.VMEM),
        *[here(t, pltpu.VMEM) for t in tabs],
    )


CORNERS = ((-1, -1), (-1, 1), (1, -1), (1, 1))
SIDES = ((-1, 0), (1, 0), (0, -1), (0, 1)) + CORNERS
CHUNK = 128
CHUNKS = ROWS_HERE // CHUNK


def margin_kernel(
    n_rows,
    n_cols,
    mask_hbm,
    wide,
    rows_in,
    cols_in,
    rows_out,
    cols_out,
    corners_out,
    chunk_in,
    chunk_out,
    in_sem,
    chunk_sem,
    store_sem,
    send_sem,
    recv_sem,
):
    row, col = lax.axis_index("trow"), lax.axis_index("tcol")

    def near(dr, dc):
        return (lax.rem(row + dr + n_rows, n_rows), lax.rem(col + dc + n_cols, n_cols))

    barrier = pltpu.get_barrier_semaphore()
    for dr, dc in SIDES:
        pl.semaphore_signal(
            barrier, inc=1, device_id=near(dr, dc), device_id_type=pl.DeviceIdType.MESH
        )

    strips = []
    for side in range(2):
        start = side * (ROWS_HERE - APRON)
        strips.append(
            pltpu.make_async_copy(
                mask_hbm.at[pl.ds(start, APRON), :], rows_in.at[side], in_sem.at[side]
            )
        )
        start = side * (COLS_HERE - SIDE)
        strips.append(
            pltpu.make_async_copy(
                mask_hbm.at[:, pl.ds(start, SIDE)], cols_in.at[side], in_sem.at[2 + side]
            )
        )
    for copy in strips:
        copy.start()

    def load(n):
        return pltpu.make_async_copy(
            mask_hbm.at[pl.ds(n * CHUNK, CHUNK), :], chunk_in.at[n % 3], chunk_sem.at[n % 3]
        )

    def store(n):
        return pltpu.make_async_copy(
            chunk_out.at[n % 2],
            wide.at[pl.ds(APRON + n * CHUNK, CHUNK), pl.ds(SIDE, COLS_HERE)],
            store_sem.at[n % 2],
        )

    load(0).start()
    load(1).start()

    inside_r = [(row > 0).astype(F32), (row < n_rows - 1).astype(F32)]
    inside_c = [(col > 0).astype(F32), (col < n_cols - 1).astype(F32)]
    for copy in strips:
        copy.wait()
    for side in range(2):
        strip = jnp.tanh(0.5 * rows_in[side]) * inside_r[side]
        rows_out[side] = strip.astype(BF)
        for other in range(2):
            cut = strip[:, :SIDE] if other == 0 else strip[:, COLS_HERE - SIDE :]
            corners_out[2 * side + other] = (cut * inside_c[other]).astype(BF)
        cols_out[side] = (jnp.tanh(0.5 * cols_in[side]) * inside_c[side]).astype(BF)

    pl.semaphore_wait(barrier, len(SIDES))

    row_place = {-1: pl.ds(APRON + ROWS_HERE, APRON), 1: pl.ds(0, APRON), 0: pl.ds(APRON, ROWS_HERE)}
    col_place = {-1: pl.ds(SIDE + COLS_HERE, SIDE), 1: pl.ds(0, SIDE), 0: pl.ds(SIDE, COLS_HERE)}
    sources = [
        rows_out.at[0],
        rows_out.at[1],
        cols_out.at[0],
        cols_out.at[1],
    ] + [corners_out.at[n] for n in range(4)]
    sends = []
    for n, (dr, dc) in enumerate(SIDES):
        sends.append(
            pltpu.make_async_remote_copy(
                src_ref=sources[n],
                dst_ref=wide.at[row_place[dr], col_place[dc]],
                send_sem=send_sem.at[n],
                recv_sem=recv_sem.at[n],
                device_id=near(dr, dc),
                device_id_type=pl.DeviceIdType.MESH,
            )
        )
    for send in sends:
        send.start()

    for n in range(CHUNKS):
        if n + 2 < CHUNKS:
            load(n + 2).start()
        load(n).wait()
        if n >= 2:
            store(n - 2).wait()
        chunk_out[n % 2] = jnp.tanh(0.5 * chunk_in[n % 3]).astype(BF)
        store(n).start()
    store(CHUNKS - 2).wait()
    store(CHUNKS - 1).wait()
    for send in sends:
        send.wait()


def widen(mask, n_rows, n_cols):
    dma = pltpu.SemaphoreType.DMA
    return pl.pallas_call(
        functools.partial(margin_kernel, n_rows, n_cols),
        out_shape=pltpu.VMEM((ROWS_HERE + 2 * APRON, COLS_HERE + 2 * SIDE), BF),
        in_specs=[pl.BlockSpec(memory_space=pltpu.HBM)],
        out_specs=pl.BlockSpec(memory_space=pltpu.VMEM),
        scratch_shapes=[
            pltpu.VMEM((2, APRON, COLS_HERE), F32),
            pltpu.VMEM((2, ROWS_HERE, SIDE), F32),
            pltpu.VMEM((2, APRON, COLS_HERE), BF),
            pltpu.VMEM((2, ROWS_HERE, SIDE), BF),
            pltpu.VMEM((4, APRON, SIDE), BF),
            pltpu.VMEM((3, CHUNK, COLS_HERE), F32),
            pltpu.VMEM((2, CHUNK, COLS_HERE), BF),
            dma((4,)),
            dma((3,)),
            dma((2,)),
            dma((len(SIDES),)),
            dma((len(SIDES),)),
        ],
        compiler_params=pltpu.CompilerParams(
            collective_id=0, has_side_effects=True, vmem_limit_bytes=32 * 1024 * 1024
        ),
        cost_estimate=pl.CostEstimate(
            flops=10_000_000, bytes_accessed=14_000_000, transcendentals=2_000_000
        ),
    )(pltpu.with_memory_space_constraint(mask, pltpu.HBM))


def body(mask_level, target, kernels, step_sizes, density_class, work_list):
    wide = widen(mask_level, lax.axis_size("trow"), lax.axis_size("tcol"))
    tabs = [jnp.asarray(t) for t in tables()]
    return take_step(density_class, step_sizes, mask_level, target, wide, kernels, tabs)


def solution(mesh):
    return jax.shard_map(
        body,
        mesh=mesh,
        in_specs=(P("trow", "tcol"), P("trow", "tcol"), P(), P(), P("trow", "tcol"), P()),
        out_specs=P("trow", "tcol"),
        check_vma=False,
    )
```

```python
import functools

import jax
import jax.numpy as jnp
import ml_dtypes
import numpy as np
from jax import lax
from jax.experimental import pallas as pl
from jax.experimental.pallas import tpu as pltpu
from jax.sharding import PartitionSpec as P

TILE = 512
APRON = 64
PAD = TILE + 2 * APRON
FREQ = 128
KERNELS = 12
MOST = 4
SLOTS = 8
GROUP = 12
LANES = 2
COLS = 4
GRID = 256
SIDE = 128
WIDE = TILE + 2 * SIDE
ROWS_HERE = 2 * TILE
COLS_HERE = COLS * TILE
BF = jnp.bfloat16
F32 = jnp.float32


def tables():
    freq = np.arange(FREQ, dtype=np.int64) - FREQ // 2

    def waves(count, period):
        turns = (freq[:, None] * np.arange(count)[None, :]) % period
        angles = turns * (2.0 * np.pi / period)
        return np.cos(angles), np.sin(angles)

    cos, sin = waves(PAD, PAD)
    spread = np.zeros((WIDE, 2 * FREQ))
    spread[SIDE - APRON : SIDE + TILE + APRON] = np.concatenate([cos, sin], 0).T
    ends = [spread[:SIDE], spread[WIDE - SIDE :]]
    edges = np.stack([np.stack([e, np.roll(e, APRON, 0)]) for e in ends])
    rows = np.concatenate([cos, sin], 0)
    cg, sg = waves(GRID, GRID)
    coarse = np.block([[cg, sg], [-sg, cg]])
    core_cos, core_sin = cos[:, APRON : APRON + TILE], sin[:, APRON : APRON + TILE]
    fine = np.block([[core_cos, core_sin], [-core_sin, core_cos]])
    back = np.concatenate([core_cos, -core_sin], 0).T
    gap = np.arange(APRON, APRON + TILE)[:, None] - np.arange(GRID)[None, :] * (PAD / GRID)
    degree = np.arange(1, FREQ)
    lift = 1.0 + 2.0 * np.cos(gap[:, :, None] * degree * (2.0 * np.pi / PAD)).sum(2)
    lift = lift / GRID
    return [
        np.ascontiguousarray(t).astype(ml_dtypes.bfloat16)
        for t in (spread, edges, rows, coarse, coarse.T, lift, lift.T, fine, back)
    ]


def dot(a, b):
    return jnp.dot(a, b, preferred_element_type=F32)


def step_kernel(
    cls_ref,
    steps_ref,
    mask_hbm,
    target_hbm,
    half_spectra,
    kern,
    rows,
    coarse,
    coarse_t,
    lift,
    lift_t,
    fine,
    back,
    out_hbm,
    slot_ref,
    goal,
    mask,
    result,
    field,
    inten,
    goal_sem,
    mask_sem,
    out_sem,
    keep_sem,
):
    count = jnp.int32(0)
    for s in range(SLOTS):
        busy = cls_ref[s // COLS, s % COLS] > 0

        @pl.when(busy)
        def _(s=s, count=count):
            slot_ref[count] = s

        count = count + busy.astype(jnp.int32)

    def corner(s):
        r, c = s // COLS, s % COLS
        return pl.multiple_of(r * TILE, TILE), pl.multiple_of(c * TILE, TILE)

    def goal_copy(i):
        r, c = corner(slot_ref[i])
        return pltpu.make_async_copy(
            target_hbm.at[pl.ds(r, TILE), pl.ds(c, TILE)], goal.at[i], goal_sem.at[i]
        )

    def mask_copy(s):
        r, c = (s // COLS) * TILE, (s % COLS) * TILE
        return pltpu.make_async_copy(
            mask_hbm.at[pl.ds(r, TILE), pl.ds(c, TILE)], mask.at[s], mask_sem.at[s]
        )

    def keep_copy(s):
        r, c = (s // COLS) * TILE, (s % COLS) * TILE
        return pltpu.make_async_copy(
            mask.at[s], out_hbm.at[pl.ds(r, TILE), pl.ds(c, TILE)], keep_sem.at[s]
        )

    def out_copy(i):
        r, c = corner(slot_ref[i])
        return pltpu.make_async_copy(
            result.at[i], out_hbm.at[pl.ds(r, TILE), pl.ds(c, TILE)], out_sem.at[i]
        )

    def fetch(i, _):
        goal_copy(i).start()
        return 0

    lax.fori_loop(0, count, fetch, 0)
    for s in range(SLOTS):
        mask_copy(s).start()

    def keep():
        for s in range(SLOTS):
            mask_copy(s).wait()

            @pl.when(cls_ref[s // COLS, s % COLS] <= 0)
            def _(s=s):
                keep_copy(s).start()

    @pl.when(count == 0)
    def _():
        keep()

    def spectrum(t):
        blocks = dot(rows[...], half_spectra[t.slot % COLS, pl.ds(t.r, PAD), :])
        re = blocks[:FREQ, :FREQ] - blocks[FREQ:, FREQ:]
        im = -(blocks[:FREQ, FREQ:] + blocks[FREQ:, :FREQ])
        t.spec_re = jnp.concatenate([re, re], 1)
        t.spec_im = jnp.concatenate([im, im], 1)

    def forward(t, k):
        parts = []
        for p in range(k, k + GROUP, 2):
            h_re = jnp.concatenate([kern[p, 0], kern[p + 1, 0]], 1)
            h_im = jnp.concatenate([kern[p, 1], kern[p + 1, 1]], 1)
            z_re = (h_re * t.spec_re - h_im * t.spec_im).astype(BF)
            z_im = (h_re * t.spec_im + h_im * t.spec_re).astype(BF)
            w = dot(coarse_t[...], jnp.concatenate([z_re, z_im], 0)).astype(BF)
            for n in range(2):
                cut = w[:, n * FREQ : (n + 1) * FREQ]
                parts.append(jnp.concatenate([cut[:GRID], cut[GRID:]], 1))
        f = dot(jnp.concatenate(parts, 0), coarse[...])
        total = None
        for n in range(GROUP):
            one = f[n * GRID : (n + 1) * GRID]
            field[t.lane, k + n] = one.astype(BF)
            square = one[:, :GRID] * one[:, :GRID] + one[:, GRID:] * one[:, GRID:]
            total = square if total is None else total + square
        if k == 0:
            inten[t.lane] = total - 1.0
        else:
            inten[t.lane] += total

    def resist(t):
        half = dot(lift[...], (2.0 * inten[t.lane]).astype(BF)).astype(BF)
        bend = jnp.tanh(dot(half, lift_t[...]))
        weight = (1.0 + bend - 2.0 * goal[t.i].astype(F32)) * (1.0 - bend * bend)
        drop = dot(lift_t[...], weight.astype(BF)).astype(BF)
        pull = (2.0 * dot(drop, lift[...])).astype(BF)
        t.pull = jnp.concatenate([pull, pull], 1)
        t.tot_re = jnp.zeros((FREQ, 2 * FREQ), F32)
        t.tot_im = jnp.zeros((FREQ, 2 * FREQ), F32)

    def adjoint(t, k):
        pulled = jnp.concatenate([field[t.lane, k + n] * t.pull for n in range(GROUP)], 0)
        x = dot(pulled, coarse_t[...]).astype(BF)
        for p in range(0, GROUP, 2):
            a = x[p * GRID : (p + 1) * GRID]
            b = x[(p + 1) * GRID : (p + 2) * GRID]
            pair = jnp.concatenate(
                [
                    jnp.concatenate([a[:, :FREQ], b[:, :FREQ]], 1),
                    jnp.concatenate([a[:, FREQ:], b[:, FREQ:]], 1),
                ],
                0,
            )
            g = dot(coarse[...], pair)
            g_re, g_im = g[:FREQ], g[FREQ:]
            h_re = jnp.concatenate([kern[k + p, 0], kern[k + p + 1, 0]], 1)
            h_im = jnp.concatenate([kern[k + p, 1], kern[k + p + 1, 1]], 1)
            t.tot_re = t.tot_re + h_re * g_re + h_im * g_im
            t.tot_im = t.tot_im + h_re * g_im - h_im * g_re

    def finish(t):
        level = cls_ref[t.slot // COLS, t.slot % COLS]
        size = 0.5 * steps_ref[level - 1]
        tot_re = size * (t.tot_re[:, :FREQ] + t.tot_re[:, FREQ:])
        tot_im = size * (t.tot_im[:, :FREQ] + t.tot_im[:, FREQ:])
        v = dot(jnp.concatenate([tot_re, tot_im], 1).astype(BF), fine[...]).astype(BF)
        grad = dot(back[...], jnp.concatenate([v[:, :TILE], v[:, TILE:]], 0))
        here = mask[t.slot]
        trans = jnp.tanh(0.5 * here)
        result[t.i] = here - grad * (1.0 - trans * trans)

    class Tile:
        def __init__(self, i, lane):
            self.i, self.lane = i, lane
            self.slot = slot_ref[i]
            self.r = pl.multiple_of(self.slot // COLS * TILE, TILE)

    def batch(b, _):
        start = b * LANES
        tiles = [Tile(jnp.minimum(start + n, count - 1), n) for n in range(LANES)]
        for t in tiles:
            spectrum(t)
        for k in range(0, KERNELS, GROUP):
            for t in tiles:
                forward(t, k)

        @pl.when(b == 0)
        def _():
            keep()
            lax.fori_loop(0, count, lambda i, _: (goal_copy(i).wait(), 0)[1], 0)

        for t in tiles:
            resist(t)
        for k in range(0, KERNELS, GROUP):
            for t in tiles:
                adjoint(t, k)
        for t in tiles:
            finish(t)
        for n in range(LANES):

            @pl.when(start + n < count)
            def _(n=n):
                out_copy(start + n).start()

        return 0

    lax.fori_loop(0, (count + LANES - 1) // LANES, batch, 0)

    lax.fori_loop(0, count, lambda i, _: (out_copy(i).wait(), 0)[1], 0)
    for s in range(SLOTS):

        @pl.when(cls_ref[s // COLS, s % COLS] <= 0)
        def _(s=s):
            keep_copy(s).wait()


def take_step(cls, steps, mask, target, half_spectra, kernels, tabs):
    hbm = pl.BlockSpec(memory_space=pltpu.HBM)
    vmem = pl.BlockSpec(memory_space=pltpu.VMEM)
    smem = pl.BlockSpec(memory_space=pltpu.SMEM)
    dma = pltpu.SemaphoreType.DMA
    here = pltpu.with_memory_space_constraint
    return pl.pallas_call(
        step_kernel,
        out_shape=jax.ShapeDtypeStruct((ROWS_HERE, COLS_HERE), F32),
        in_specs=[smem, smem, hbm, hbm, vmem, vmem] + [vmem] * len(tabs),
        out_specs=hbm,
        scratch_shapes=[
            pltpu.SMEM((SLOTS,), jnp.int32),
            pltpu.VMEM((MOST, TILE, TILE), BF),
            pltpu.VMEM((SLOTS, TILE, TILE), F32),
            pltpu.VMEM((MOST, TILE, TILE), F32),
            pltpu.VMEM((LANES, KERNELS, GRID, 2 * GRID), BF),
            pltpu.VMEM((LANES, GRID, GRID), F32),
            dma((MOST,)),
            dma((SLOTS,)),
            dma((MOST,)),
            dma((SLOTS,)),
        ],
        compiler_params=pltpu.CompilerParams(vmem_limit_bytes=48 * 1024 * 1024),
        cost_estimate=pl.CostEstimate(
            flops=30_000_000_000, bytes_accessed=40_000_000, transcendentals=3_000_000
        ),
    )(
        cls,
        steps,
        here(mask, pltpu.HBM),
        here(target, pltpu.HBM),
        here(half_spectra, pltpu.VMEM),
        here(kernels, pltpu.VMEM),
        *[here(t, pltpu.VMEM) for t in tabs],
    )


CORNERS = ((-1, -1), (-1, 1), (1, -1), (1, 1))
SIDES = ((-1, 0), (1, 0), (0, -1), (0, 1)) + CORNERS
CHUNK = 256
CHUNKS = ROWS_HERE // CHUNK
HALF = ROWS_HERE // 2


def near_transform(trans, spread):
    pieces = []
    for c in range(COLS):
        first, last = c * TILE - SIDE, (c + 1) * TILE + SIDE
        low, high = max(first, 0), min(last, COLS_HERE)
        pieces.append(dot(trans[:, low:high], spread[low - first : high - first, :]))
    return pieces


def margin_kernel(
    n_rows,
    n_cols,
    mask_hbm,
    spread,
    edges,
    out,
    mask,
    rows_out,
    cols_out,
    corners_out,
    rows_got,
    cols_got,
    corners_got,
    part,
    strip_sem,
    chunk_sem,
    send_sem,
    recv_sem,
):
    row, col = lax.axis_index("trow"), lax.axis_index("tcol")

    def near(dr, dc):
        return (lax.rem(row + dr + n_rows, n_rows), lax.rem(col + dc + n_cols, n_cols))

    barrier = pltpu.get_barrier_semaphore()
    for dr, dc in SIDES:
        pl.semaphore_signal(
            barrier, inc=1, device_id=near(dr, dc), device_id_type=pl.DeviceIdType.MESH
        )

    def load(r, height, c, width, sem):
        where = (pl.ds(r, height), pl.ds(c, width))
        return pltpu.make_async_copy(mask_hbm.at[where], mask.at[where], sem)

    inner = ROWS_HERE - 2 * APRON
    strips = [
        load(0, APRON, 0, COLS_HERE, strip_sem.at[0]),
        load(ROWS_HERE - APRON, APRON, 0, COLS_HERE, strip_sem.at[1]),
        load(APRON, inner, 0, SIDE, strip_sem.at[2]),
        load(APRON, inner, COLS_HERE - SIDE, SIDE, strip_sem.at[3]),
    ]
    chunks = []
    for n in range(CHUNKS):
        top = max(n * CHUNK, APRON)
        height = min((n + 1) * CHUNK, ROWS_HERE - APRON) - top
        chunks.append(load(top, height, SIDE, COLS_HERE - 2 * SIDE, chunk_sem.at[n]))
    for copy in strips + chunks:
        copy.start()

    inside_r = [(row > 0).astype(F32), (row < n_rows - 1).astype(F32)]
    inside_c = [(col > 0).astype(F32), (col < n_cols - 1).astype(F32)]

    strips[0].wait()
    strips[1].wait()
    bands = []
    for side in range(2):
        start = side * (ROWS_HERE - APRON)
        band = jnp.tanh(0.5 * mask[start : start + APRON, :]) * inside_r[side]
        bands.append(band.astype(BF))
        for other in range(2):
            begin = other * (COLS_HERE - SIDE)
            cut = band[:, begin : begin + SIDE] * inside_c[other]
            corners_out[2 * side + other] = cut.astype(BF)
    for c, piece in enumerate(near_transform(jnp.concatenate(bands, 0), spread)):
        for side in range(2):
            rows_out[side, c] = piece[side * APRON : (side + 1) * APRON].astype(BF)

    strips[2].wait()
    strips[3].wait()
    left_lanes = lax.broadcasted_iota(jnp.int32, (HALF, SIDE), 1) < APRON
    for side in range(2):
        start = side * (COLS_HERE - SIDE)
        band = jnp.tanh(0.5 * mask[:, start : start + SIDE]) * inside_c[side]
        upper, lower = band[:HALF], pltpu.roll(band[HALF:], APRON, 1)
        if side == 1:
            upper, lower = lower, upper
        cols_out[side] = jnp.where(left_lanes, upper, lower).astype(BF)

    sources = [rows_out.at[0], rows_out.at[1], cols_out.at[0], cols_out.at[1]]
    places = [rows_got.at[1], rows_got.at[0], cols_got.at[1], cols_got.at[0]]
    for n in range(len(CORNERS)):
        sources.append(corners_out.at[n])
        places.append(corners_got.at[len(CORNERS) - 1 - n])
    sends = [
        pltpu.make_async_remote_copy(
            src_ref=sources[n],
            dst_ref=places[n],
            send_sem=send_sem.at[n],
            recv_sem=recv_sem.at[n],
            device_id=near(dr, dc),
            device_id_type=pl.DeviceIdType.MESH,
        )
        for n, (dr, dc) in enumerate(SIDES)
    ]
    pl.semaphore_wait(barrier, len(SIDES))
    for send in sends:
        send.start()

    for n in range(CHUNKS):
        chunks[n].wait()
        here = slice(n * CHUNK, (n + 1) * CHUNK)
        pieces = near_transform(jnp.tanh(0.5 * mask[here, :]).astype(BF), spread)
        part[0, here] = pieces[0]
        part[1, here] = pieces[-1]
        for c in range(1, COLS - 1):
            out[c, APRON + n * CHUNK : APRON + (n + 1) * CHUNK] = pieces[c].astype(BF)

    sends[2].wait()
    sends[3].wait()
    for side, c in ((0, 0), (1, COLS - 1)):
        for h in range(2):
            here = slice(h * HALF, (h + 1) * HALF)
            whole = part[side, here] + dot(cols_got[side], edges[side, h])
            out[c, APRON + h * HALF : APRON + (h + 1) * HALF] = whole.astype(BF)
    sends[0].wait()
    sends[1].wait()
    for send in sends[4:]:
        send.wait()
    for side in range(2):
        start = side * (APRON + ROWS_HERE)
        for c in range(COLS):
            value = rows_got[side, c]
            other = {0: 0, COLS - 1: 1}.get(c)
            if other is not None:
                corner = dot(corners_got[2 * side + other], edges[other, 0])
                value = (value.astype(F32) + corner).astype(BF)
            out[c, start : start + APRON] = value


def half_transform(mask, spread, edges, n_rows, n_cols):
    vmem = pl.BlockSpec(memory_space=pltpu.VMEM)
    dma = pltpu.SemaphoreType.DMA
    here = pltpu.with_memory_space_constraint
    rows_shape = (2, COLS, APRON, 2 * FREQ)
    cols_shape = (2, HALF, SIDE)
    corners_shape = (len(CORNERS), APRON, SIDE)
    return pl.pallas_call(
        functools.partial(margin_kernel, n_rows, n_cols),
        out_shape=pltpu.VMEM((COLS, ROWS_HERE + 2 * APRON, 2 * FREQ), BF),
        in_specs=[pl.BlockSpec(memory_space=pltpu.HBM), vmem, vmem],
        out_specs=vmem,
        scratch_shapes=[
            pltpu.VMEM((ROWS_HERE, COLS_HERE), F32),
            pltpu.VMEM(rows_shape, BF),
            pltpu.VMEM(cols_shape, BF),
            pltpu.VMEM(corners_shape, BF),
            pltpu.VMEM(rows_shape, BF),
            pltpu.VMEM(cols_shape, BF),
            pltpu.VMEM(corners_shape, BF),
            pltpu.VMEM((2, ROWS_HERE, 2 * FREQ), F32),
            dma((4,)),
            dma((CHUNKS,)),
            dma((len(SIDES),)),
            dma((len(SIDES),)),
        ],
        compiler_params=pltpu.CompilerParams(
            collective_id=0, has_side_effects=True, vmem_limit_bytes=40 * 1024 * 1024
        ),
        cost_estimate=pl.CostEstimate(
            flops=2_000_000_000, bytes_accessed=10_000_000, transcendentals=2_000_000
        ),
    )(here(mask, pltpu.HBM), here(spread, pltpu.VMEM), here(edges, pltpu.VMEM))


def body(mask_level, target, kernels, step_sizes, density_class, work_list):
    spread, edges, *tabs = [jnp.asarray(t) for t in tables()]
    half_spectra = half_transform(
        mask_level, spread, edges, lax.axis_size("trow"), lax.axis_size("tcol")
    )
    return take_step(density_class, step_sizes, mask_level, target, half_spectra, kernels, tabs)


def solution(mesh):
    return jax.shard_map(
        body,
        mesh=mesh,
        in_specs=(P("trow", "tcol"), P("trow", "tcol"), P(), P(), P("trow", "tcol"), P()),
        out_specs=P("trow", "tcol"),
        check_vma=False,
    )
```

```python
import functools

import jax
import jax.numpy as jnp
import ml_dtypes
import numpy as np
from jax import lax
from jax.experimental import pallas as pl
from jax.experimental.pallas import tpu as pltpu
from jax.sharding import PartitionSpec as P

TILE = 512
APRON = 64
PAD = TILE + 2 * APRON
FREQ = 128
KERNELS = 12
MOST = 4
SLOTS = 8
LANES = 2
PART = 512
COLS = 4
GRID = 256
SIDE = 128
WIDE = TILE + 2 * SIDE
ROWS_HERE = 2 * TILE
COLS_HERE = COLS * TILE
BF = jnp.bfloat16
F32 = jnp.float32


def tables():
    freq = np.arange(FREQ, dtype=np.int64) - FREQ // 2

    def waves(count, period):
        turns = (freq[:, None] * np.arange(count)[None, :]) % period
        angles = turns * (2.0 * np.pi / period)
        return np.cos(angles), np.sin(angles)

    cos, sin = waves(PAD, PAD)
    spread = np.zeros((WIDE, 2 * FREQ))
    spread[SIDE - APRON : SIDE + TILE + APRON] = np.concatenate([cos, sin], 0).T
    ends = [spread[:SIDE], spread[WIDE - SIDE :]]
    edges = np.stack([np.stack([e, np.roll(e, APRON, 0)]) for e in ends])
    rows = np.concatenate([cos, sin], 0)
    cg, sg = waves(GRID, GRID)
    coarse = np.block([[cg, sg], [-sg, cg]])
    core_cos, core_sin = cos[:, APRON : APRON + TILE], sin[:, APRON : APRON + TILE]
    fine = np.block([[core_cos, core_sin], [-core_sin, core_cos]])
    back = np.concatenate([core_cos, -core_sin], 0).T
    gap = np.arange(APRON, APRON + TILE)[:, None] - np.arange(GRID)[None, :] * (PAD / GRID)
    degree = np.arange(1, FREQ)
    lift = 1.0 + 2.0 * np.cos(gap[:, :, None] * degree * (2.0 * np.pi / PAD)).sum(2)
    lift = lift / GRID
    return [
        np.ascontiguousarray(t).astype(ml_dtypes.bfloat16)
        for t in (spread, edges, rows, coarse, coarse.T, lift, lift.T, fine, back)
    ]


def dot(a, b):
    return jnp.dot(a, b, preferred_element_type=F32)


def step_kernel(
    cls_ref,
    steps_ref,
    mask_hbm,
    target_hbm,
    half_spectra,
    kern,
    rows,
    coarse,
    coarse_t,
    lift,
    lift_t,
    fine,
    back,
    out_hbm,
    slot_ref,
    goal,
    mask,
    result,
    field,
    inten,
    goal_sem,
    mask_sem,
    out_sem,
    keep_sem,
):
    count = jnp.int32(0)
    for s in range(SLOTS):
        busy = cls_ref[s // COLS, s % COLS] > 0

        @pl.when(busy)
        def _(s=s, count=count):
            slot_ref[count] = s

        count = count + busy.astype(jnp.int32)

    def corner(s):
        r, c = s // COLS, s % COLS
        return pl.multiple_of(r * TILE, TILE), pl.multiple_of(c * TILE, TILE)

    def goal_copy(i):
        r, c = corner(slot_ref[i])
        return pltpu.make_async_copy(
            target_hbm.at[pl.ds(r, TILE), pl.ds(c, TILE)], goal.at[i], goal_sem.at[i]
        )

    def mask_copy(s):
        r, c = (s // COLS) * TILE, (s % COLS) * TILE
        return pltpu.make_async_copy(
            mask_hbm.at[pl.ds(r, TILE), pl.ds(c, TILE)], mask.at[s], mask_sem.at[s]
        )

    def keep_copy(s):
        r, c = (s // COLS) * TILE, (s % COLS) * TILE
        return pltpu.make_async_copy(
            mask.at[s], out_hbm.at[pl.ds(r, TILE), pl.ds(c, TILE)], keep_sem.at[s]
        )

    def out_copy(i):
        r, c = corner(slot_ref[i])
        return pltpu.make_async_copy(
            result.at[i], out_hbm.at[pl.ds(r, TILE), pl.ds(c, TILE)], out_sem.at[i]
        )

    def fetch(i, _):
        goal_copy(i).start()
        return 0

    lax.fori_loop(0, count, fetch, 0)
    for s in range(SLOTS):
        mask_copy(s).start()

    def keep():
        for s in range(SLOTS):
            mask_copy(s).wait()

            @pl.when(cls_ref[s // COLS, s % COLS] <= 0)
            def _(s=s):
                keep_copy(s).start()

    @pl.when(count == 0)
    def _():
        keep()

    def spectrum(t):
        blocks = dot(rows[...], half_spectra[t.slot % COLS, pl.ds(t.r, PAD), :])
        re = blocks[:FREQ, :FREQ] - blocks[FREQ:, FREQ:]
        im = -(blocks[:FREQ, FREQ:] + blocks[FREQ:, :FREQ])
        t.spec_re, t.spec_im = re, im

    def kernel_lanes(part):
        return jnp.concatenate([kern[k, part] for k in range(KERNELS)], 1)

    def forward(t, _):
        h_re, h_im = kernel_lanes(0), kernel_lanes(1)
        re = jnp.concatenate([t.spec_re] * KERNELS, 1)
        im = jnp.concatenate([t.spec_im] * KERNELS, 1)
        z_re = (h_re * re - h_im * im).astype(BF)
        z_im = (h_re * im + h_im * re).astype(BF)
        w = dot(coarse_t[...], jnp.concatenate([z_re, z_im], 0)).astype(BF)
        parts = []
        for k in range(KERNELS):
            cut = w[:, k * FREQ : (k + 1) * FREQ]
            parts.append(jnp.concatenate([cut[:GRID], cut[GRID:]], 1))
        f = dot(jnp.concatenate(parts, 0), coarse[...])
        total = None
        for k in range(KERNELS):
            one = f[k * GRID : (k + 1) * GRID]
            field[t.lane, k] = one.astype(BF)
            square = one[:, :GRID] * one[:, :GRID] + one[:, GRID:] * one[:, GRID:]
            total = square if total is None else total + square
        inten[t.lane] = total - 1.0

    def resist(t):
        half = dot(lift[...], (2.0 * inten[t.lane]).astype(BF)).astype(BF)
        bend = jnp.tanh(dot(half, lift_t[...]))
        weight = (1.0 + bend - 2.0 * goal[t.i].astype(F32)) * (1.0 - bend * bend)
        drop = dot(lift_t[...], weight.astype(BF)).astype(BF)
        pull = (2.0 * dot(drop, lift[...])).astype(BF)
        t.pull = jnp.concatenate([pull, pull], 1)

    def adjoint(t, _):
        pulled = jnp.concatenate([field[t.lane, k] * t.pull for k in range(KERNELS)], 0)
        x = jnp.concatenate(
            [
                dot(pulled[m : m + PART], coarse_t[...]).astype(BF)
                for m in range(0, KERNELS * GRID, PART)
            ],
            0,
        )
        wide = jnp.concatenate(
            [
                jnp.concatenate(
                    [
                        x[k * GRID : (k + 1) * GRID, part * FREQ : (part + 1) * FREQ]
                        for k in range(KERNELS)
                    ],
                    1,
                )
                for part in range(2)
            ],
            0,
        )
        g = jnp.concatenate(
            [
                dot(coarse[...], wide[:, m : m + PART])
                for m in range(0, KERNELS * FREQ, PART)
            ],
            1,
        )
        tot_re = tot_im = None
        for k in range(KERNELS):
            cut = g[:, k * FREQ : (k + 1) * FREQ]
            g_re, g_im = cut[:FREQ], cut[FREQ:]
            h_re, h_im = kern[k, 0], kern[k, 1]
            one_re = h_re * g_re + h_im * g_im
            one_im = h_re * g_im - h_im * g_re
            tot_re = one_re if k == 0 else tot_re + one_re
            tot_im = one_im if k == 0 else tot_im + one_im
        t.tot_re, t.tot_im = tot_re, tot_im

    def finish(t):
        level = cls_ref[t.slot // COLS, t.slot % COLS]
        size = 0.5 * steps_ref[level - 1]
        tot_re = size * t.tot_re
        tot_im = size * t.tot_im
        v = dot(jnp.concatenate([tot_re, tot_im], 1).astype(BF), fine[...]).astype(BF)
        grad = dot(back[...], jnp.concatenate([v[:, :TILE], v[:, TILE:]], 0))
        here = mask[t.slot]
        trans = jnp.tanh(0.5 * here)
        result[t.i] = here - grad * (1.0 - trans * trans)

    class Tile:
        def __init__(self, i, lane):
            self.i, self.lane = i, lane
            self.slot = slot_ref[i]
            self.r = pl.multiple_of(self.slot // COLS * TILE, TILE)

    def batch(b, _):
        start = b * LANES
        tiles = [Tile(jnp.minimum(start + n, count - 1), n) for n in range(LANES)]
        for t in tiles:
            spectrum(t)
        for t in tiles:
            forward(t, 0)

        @pl.when(b == 0)
        def _():
            keep()
            lax.fori_loop(0, count, lambda i, _: (goal_copy(i).wait(), 0)[1], 0)

        for t in tiles:
            resist(t)
        for t in tiles:
            adjoint(t, 0)
        for t in tiles:
            finish(t)
        for n in range(LANES):

            @pl.when(start + n < count)
            def _(n=n):
                out_copy(start + n).start()

        return 0

    lax.fori_loop(0, (count + LANES - 1) // LANES, batch, 0)

    lax.fori_loop(0, count, lambda i, _: (out_copy(i).wait(), 0)[1], 0)
    for s in range(SLOTS):

        @pl.when(cls_ref[s // COLS, s % COLS] <= 0)
        def _(s=s):
            keep_copy(s).wait()


def take_step(cls, steps, mask, target, half_spectra, kernels, tabs):
    hbm = pl.BlockSpec(memory_space=pltpu.HBM)
    vmem = pl.BlockSpec(memory_space=pltpu.VMEM)
    smem = pl.BlockSpec(memory_space=pltpu.SMEM)
    dma = pltpu.SemaphoreType.DMA
    here = pltpu.with_memory_space_constraint
    return pl.pallas_call(
        step_kernel,
        out_shape=jax.ShapeDtypeStruct((ROWS_HERE, COLS_HERE), F32),
        in_specs=[smem, smem, hbm, hbm, vmem, vmem] + [vmem] * len(tabs),
        out_specs=hbm,
        scratch_shapes=[
            pltpu.SMEM((SLOTS,), jnp.int32),
            pltpu.VMEM((MOST, TILE, TILE), BF),
            pltpu.VMEM((SLOTS, TILE, TILE), F32),
            pltpu.VMEM((MOST, TILE, TILE), F32),
            pltpu.VMEM((LANES, KERNELS, GRID, 2 * GRID), BF),
            pltpu.VMEM((LANES, GRID, GRID), F32),
            dma((MOST,)),
            dma((SLOTS,)),
            dma((MOST,)),
            dma((SLOTS,)),
        ],
        compiler_params=pltpu.CompilerParams(vmem_limit_bytes=48 * 1024 * 1024),
        cost_estimate=pl.CostEstimate(
            flops=30_000_000_000, bytes_accessed=40_000_000, transcendentals=3_000_000
        ),
    )(
        cls,
        steps,
        here(mask, pltpu.HBM),
        here(target, pltpu.HBM),
        here(half_spectra, pltpu.VMEM),
        here(kernels, pltpu.VMEM),
        *[here(t, pltpu.VMEM) for t in tabs],
    )


CORNERS = ((-1, -1), (-1, 1), (1, -1), (1, 1))
SIDES = ((-1, 0), (1, 0), (0, -1), (0, 1)) + CORNERS
CHUNK = 256
CHUNKS = ROWS_HERE // CHUNK
HALF = ROWS_HERE // 2


def near_transform(trans, spread):
    pieces = []
    for c in range(COLS):
        first, last = c * TILE - SIDE, (c + 1) * TILE + SIDE
        low, high = max(first, 0), min(last, COLS_HERE)
        pieces.append(dot(trans[:, low:high], spread[low - first : high - first, :]))
    return pieces


def margin_kernel(
    n_rows,
    n_cols,
    mask_hbm,
    spread_hbm,
    edges_hbm,
    out,
    mask,
    spread,
    edges,
    rows_out,
    cols_out,
    corners_out,
    rows_got,
    cols_got,
    corners_got,
    part,
    strip_sem,
    table_sem,
    chunk_sem,
    send_sem,
    recv_sem,
):
    row, col = lax.axis_index("trow"), lax.axis_index("tcol")

    def near(dr, dc):
        return (lax.rem(row + dr + n_rows, n_rows), lax.rem(col + dc + n_cols, n_cols))

    barrier = pltpu.get_barrier_semaphore()
    for dr, dc in SIDES:
        pl.semaphore_signal(
            barrier, inc=1, device_id=near(dr, dc), device_id_type=pl.DeviceIdType.MESH
        )

    def load(r, height, c, width, sem):
        where = (pl.ds(r, height), pl.ds(c, width))
        return pltpu.make_async_copy(mask_hbm.at[where], mask.at[where], sem)

    inner = ROWS_HERE - 2 * APRON
    strips = [
        load(0, APRON, 0, COLS_HERE, strip_sem.at[0]),
        load(ROWS_HERE - APRON, APRON, 0, COLS_HERE, strip_sem.at[1]),
        load(APRON, inner, 0, SIDE, strip_sem.at[2]),
        load(APRON, inner, COLS_HERE - SIDE, SIDE, strip_sem.at[3]),
    ]
    chunks = []
    for n in range(CHUNKS):
        top = max(n * CHUNK, APRON)
        height = min((n + 1) * CHUNK, ROWS_HERE - APRON) - top
        chunks.append(load(top, height, SIDE, COLS_HERE - 2 * SIDE, chunk_sem.at[n]))
    near_table = pltpu.make_async_copy(spread_hbm, spread, table_sem.at[0])
    edge_table = pltpu.make_async_copy(edges_hbm, edges, table_sem.at[1])
    for copy in strips[:2] + [near_table] + strips[2:] + chunks[:1] + [edge_table] + chunks[1:]:
        copy.start()

    inside_r = [(row > 0).astype(F32), (row < n_rows - 1).astype(F32)]
    inside_c = [(col > 0).astype(F32), (col < n_cols - 1).astype(F32)]

    def packed(band, side):
        half = band.shape[0] // 2
        upper, lower = band[:half], pltpu.roll(band[half:], APRON, 1)
        if side == 1:
            upper, lower = lower, upper
        lane = lax.broadcasted_iota(jnp.int32, (half, SIDE), 1)
        return jnp.where(lane < APRON, upper, lower).astype(BF)

    strips[0].wait()
    strips[1].wait()
    bands = []
    for side in range(2):
        start = side * (ROWS_HERE - APRON)
        band = jnp.tanh(0.5 * mask[start : start + APRON, :]) * inside_r[side]
        bands.append(band.astype(BF))
        for other in range(2):
            begin = other * (COLS_HERE - SIDE)
            cut = band[:, begin : begin + SIDE] * inside_c[other]
            corners_out[2 * side + other] = packed(cut, other)
    near_table.wait()
    for c, piece in enumerate(near_transform(jnp.concatenate(bands, 0), spread)):
        for side in range(2):
            rows_out[side, c] = piece[side * APRON : (side + 1) * APRON].astype(BF)

    sources = [rows_out.at[0], rows_out.at[1], cols_out.at[0], cols_out.at[1]]
    places = [rows_got.at[1], rows_got.at[0], cols_got.at[1], cols_got.at[0]]
    for n in range(len(CORNERS)):
        sources.append(corners_out.at[n])
        places.append(corners_got.at[len(CORNERS) - 1 - n])
    sends = [
        pltpu.make_async_remote_copy(
            src_ref=sources[n],
            dst_ref=places[n],
            send_sem=send_sem.at[n],
            recv_sem=recv_sem.at[n],
            device_id=near(dr, dc),
            device_id_type=pl.DeviceIdType.MESH,
        )
        for n, (dr, dc) in enumerate(SIDES)
    ]
    pl.semaphore_wait(barrier, len(SIDES))
    for send in sends[:2] + sends[4:]:
        send.start()

    strips[2].wait()
    strips[3].wait()
    for side in range(2):
        start = side * (COLS_HERE - SIDE)
        band = jnp.tanh(0.5 * mask[:, start : start + SIDE]) * inside_c[side]
        cols_out[side] = packed(band, side)
    for send in sends[2:4]:
        send.start()

    for n in range(CHUNKS):
        chunks[n].wait()
        here = slice(n * CHUNK, (n + 1) * CHUNK)
        pieces = near_transform(jnp.tanh(0.5 * mask[here, :]).astype(BF), spread)
        part[0, here] = pieces[0]
        part[1, here] = pieces[-1]
        for c in range(1, COLS - 1):
            out[c, APRON + n * CHUNK : APRON + (n + 1) * CHUNK] = pieces[c].astype(BF)

    edge_table.wait()
    sends[2].wait()
    sends[3].wait()
    for side, c in ((0, 0), (1, COLS - 1)):
        for h in range(2):
            here = slice(h * HALF, (h + 1) * HALF)
            whole = part[side, here] + dot(cols_got[side], edges[side, h])
            out[c, APRON + h * HALF : APRON + (h + 1) * HALF] = whole.astype(BF)
    sends[0].wait()
    sends[1].wait()
    for send in sends[4:]:
        send.wait()
    for side in range(2):
        start = side * (APRON + ROWS_HERE)
        for c in range(COLS):
            value = rows_got[side, c]
            other = {0: 0, COLS - 1: 1}.get(c)
            if other is not None:
                got = corners_got[2 * side + other]
                corner = [dot(got, edges[other, h]) for h in range(2)]
                corner = jnp.concatenate(corner, 0)
                value = (value.astype(F32) + corner).astype(BF)
            out[c, start : start + APRON] = value


def half_transform(mask, spread, edges, n_rows, n_cols):
    vmem = pl.BlockSpec(memory_space=pltpu.VMEM)
    dma = pltpu.SemaphoreType.DMA
    here = pltpu.with_memory_space_constraint
    rows_shape = (2, COLS, APRON, 2 * FREQ)
    cols_shape = (2, HALF, SIDE)
    corners_shape = (len(CORNERS), APRON // 2, SIDE)
    return pl.pallas_call(
        functools.partial(margin_kernel, n_rows, n_cols),
        out_shape=pltpu.VMEM((COLS, ROWS_HERE + 2 * APRON, 2 * FREQ), BF),
        in_specs=[pl.BlockSpec(memory_space=pltpu.HBM)] * 3,
        out_specs=vmem,
        scratch_shapes=[
            pltpu.VMEM((ROWS_HERE, COLS_HERE), F32),
            pltpu.VMEM((WIDE, 2 * FREQ), BF),
            pltpu.VMEM((2, 2, SIDE, 2 * FREQ), BF),
            pltpu.VMEM(rows_shape, BF),
            pltpu.VMEM(cols_shape, BF),
            pltpu.VMEM(corners_shape, BF),
            pltpu.VMEM(rows_shape, BF),
            pltpu.VMEM(cols_shape, BF),
            pltpu.VMEM(corners_shape, BF),
            pltpu.VMEM((2, ROWS_HERE, 2 * FREQ), F32),
            dma((4,)),
            dma((2,)),
            dma((CHUNKS,)),
            dma((len(SIDES),)),
            dma((len(SIDES),)),
        ],
        compiler_params=pltpu.CompilerParams(
            collective_id=0, has_side_effects=True, vmem_limit_bytes=40 * 1024 * 1024
        ),
        cost_estimate=pl.CostEstimate(
            flops=2_000_000_000, bytes_accessed=10_000_000, transcendentals=2_000_000
        ),
    )(*[here(a, pltpu.HBM) for a in (mask, spread, edges)])


def body(mask_level, target, kernels, step_sizes, density_class, work_list):
    spread, edges, *tabs = [jnp.asarray(t) for t in tables()]
    half_spectra = half_transform(
        mask_level, spread, edges, lax.axis_size("trow"), lax.axis_size("tcol")
    )
    return take_step(density_class, step_sizes, mask_level, target, half_spectra, kernels, tabs)


def solution(mesh):
    return jax.shard_map(
        body,
        mesh=mesh,
        in_specs=(P("trow", "tcol"), P("trow", "tcol"), P(), P(), P("trow", "tcol"), P()),
        out_specs=P("trow", "tcol"),
        check_vma=False,
    )
```

```python
import functools

import jax
import jax.numpy as jnp
import ml_dtypes
import numpy as np
from jax import lax
from jax.experimental import pallas as pl
from jax.experimental.pallas import tpu as pltpu
from jax.sharding import PartitionSpec as P

TILE = 512
APRON = 64
PAD = TILE + 2 * APRON
FREQ = 128
KERNELS = 12
MOST = 4
SLOTS = 8
LANES = 2
PART = 512
COLS = 4
GRID = 256
SIDE = 128
WIDE = TILE + 2 * SIDE
ROWS_HERE = 2 * TILE
COLS_HERE = COLS * TILE
BF = jnp.bfloat16
F32 = jnp.float32


def tables():
    freq = np.arange(FREQ, dtype=np.int64) - FREQ // 2

    def waves(count, period):
        turns = (freq[:, None] * np.arange(count)[None, :]) % period
        angles = turns * (2.0 * np.pi / period)
        return np.cos(angles), np.sin(angles)

    cos, sin = waves(PAD, PAD)
    spread = np.zeros((WIDE, 2 * FREQ))
    spread[SIDE - APRON : SIDE + TILE + APRON] = np.concatenate([cos, sin], 0).T
    ends = [spread[:SIDE], spread[WIDE - SIDE :]]
    edges = np.stack([np.stack([e, np.roll(e, APRON, 0)]) for e in ends])
    rows = np.concatenate([cos, sin], 0)
    half = FREQ // 2
    mirror = np.zeros((2 * FREQ, 2 * FREQ))
    for n in range(half):
        mirror[n, n] = mirror[half + n, FREQ + n] = 1.0
        if n:
            mirror[n, FREQ - n] = 1.0
            mirror[half + n, 2 * FREQ - n] = -1.0
    mirror[FREQ:, half] = 1.0
    cg, sg = waves(GRID, GRID)
    coarse = np.block([[cg, sg], [-sg, cg]])
    core_cos, core_sin = cos[:, APRON : APRON + TILE], sin[:, APRON : APRON + TILE]
    fine = np.block([[core_cos, core_sin], [-core_sin, core_cos]])
    back = np.concatenate([core_cos, -core_sin], 0).T
    gap = np.arange(APRON, APRON + TILE)[:, None] - np.arange(GRID)[None, :] * (PAD / GRID)
    degree = np.arange(1, FREQ)
    lift = 1.0 + 2.0 * np.cos(gap[:, :, None] * degree * (2.0 * np.pi / PAD)).sum(2)
    lift = lift / GRID
    return [
        np.ascontiguousarray(t).astype(ml_dtypes.bfloat16)
        for t in (spread, edges, mirror, rows, coarse, coarse.T, lift, lift.T, fine, back)
    ]


def dot(a, b):
    return jnp.dot(a, b, preferred_element_type=F32)


def step_kernel(
    cls_ref,
    steps_ref,
    mask_hbm,
    target_hbm,
    half_spectra,
    kern,
    rows,
    coarse,
    coarse_t,
    lift,
    lift_t,
    fine,
    back,
    out_hbm,
    slot_ref,
    goal,
    mask,
    result,
    field,
    inten,
    goal_sem,
    mask_sem,
    out_sem,
    keep_sem,
):
    count = jnp.int32(0)
    for s in range(SLOTS):
        busy = cls_ref[s // COLS, s % COLS] > 0

        @pl.when(busy)
        def _(s=s, count=count):
            slot_ref[count] = s

        count = count + busy.astype(jnp.int32)

    def corner(s):
        r, c = s // COLS, s % COLS
        return pl.multiple_of(r * TILE, TILE), pl.multiple_of(c * TILE, TILE)

    def goal_copy(i):
        r, c = corner(slot_ref[i])
        return pltpu.make_async_copy(
            target_hbm.at[pl.ds(r, TILE), pl.ds(c, TILE)], goal.at[i], goal_sem.at[i]
        )

    def mask_copy(s):
        r, c = (s // COLS) * TILE, (s % COLS) * TILE
        return pltpu.make_async_copy(
            mask_hbm.at[pl.ds(r, TILE), pl.ds(c, TILE)], mask.at[s], mask_sem.at[s]
        )

    def keep_copy(s):
        r, c = (s // COLS) * TILE, (s % COLS) * TILE
        return pltpu.make_async_copy(
            mask.at[s], out_hbm.at[pl.ds(r, TILE), pl.ds(c, TILE)], keep_sem.at[s]
        )

    def out_copy(i):
        r, c = corner(slot_ref[i])
        return pltpu.make_async_copy(
            result.at[i], out_hbm.at[pl.ds(r, TILE), pl.ds(c, TILE)], out_sem.at[i]
        )

    def fetch(i, _):
        goal_copy(i).start()
        return 0

    lax.fori_loop(0, count, fetch, 0)
    for s in range(SLOTS):
        mask_copy(s).start()

    def keep():
        for s in range(SLOTS):
            mask_copy(s).wait()

            @pl.when(cls_ref[s // COLS, s % COLS] <= 0)
            def _(s=s):
                keep_copy(s).start()

    @pl.when(count == 0)
    def _():
        keep()

    def spectrum(t):
        blocks = dot(rows[...], half_spectra[t.slot % COLS, pl.ds(t.r, PAD), :])
        re = blocks[:FREQ, :FREQ] - blocks[FREQ:, FREQ:]
        im = -(blocks[:FREQ, FREQ:] + blocks[FREQ:, :FREQ])
        t.spec_re, t.spec_im = re, im

    def kernel_lanes(part):
        return jnp.concatenate([kern[k, part] for k in range(KERNELS)], 1)

    def forward(t, _):
        h_re, h_im = kernel_lanes(0), kernel_lanes(1)
        re = jnp.concatenate([t.spec_re] * KERNELS, 1)
        im = jnp.concatenate([t.spec_im] * KERNELS, 1)
        z_re = (h_re * re - h_im * im).astype(BF)
        z_im = (h_re * im + h_im * re).astype(BF)
        w = dot(coarse_t[...], jnp.concatenate([z_re, z_im], 0)).astype(BF)
        parts = []
        for k in range(KERNELS):
            cut = w[:, k * FREQ : (k + 1) * FREQ]
            parts.append(jnp.concatenate([cut[:GRID], cut[GRID:]], 1))
        f = dot(jnp.concatenate(parts, 0), coarse[...])
        total = None
        for k in range(KERNELS):
            one = f[k * GRID : (k + 1) * GRID]
            field[t.lane, k] = one.astype(BF)
            square = one[:, :GRID] * one[:, :GRID] + one[:, GRID:] * one[:, GRID:]
            total = square if total is None else total + square
        inten[t.lane] = total - 1.0

    def resist(t):
        half = dot(lift[...], (2.0 * inten[t.lane]).astype(BF)).astype(BF)
        bend = jnp.tanh(dot(half, lift_t[...]))
        weight = (1.0 + bend - 2.0 * goal[t.i].astype(F32)) * (1.0 - bend * bend)
        drop = dot(lift_t[...], weight.astype(BF)).astype(BF)
        pull = (2.0 * dot(drop, lift[...])).astype(BF)
        t.pull = jnp.concatenate([pull, pull], 1)

    def adjoint(t, _):
        pulled = jnp.concatenate([field[t.lane, k] * t.pull for k in range(KERNELS)], 0)
        x = jnp.concatenate(
            [
                dot(pulled[m : m + PART], coarse_t[...]).astype(BF)
                for m in range(0, KERNELS * GRID, PART)
            ],
            0,
        )
        wide = jnp.concatenate(
            [
                jnp.concatenate(
                    [
                        x[k * GRID : (k + 1) * GRID, part * FREQ : (part + 1) * FREQ]
                        for k in range(KERNELS)
                    ],
                    1,
                )
                for part in range(2)
            ],
            0,
        )
        g = jnp.concatenate(
            [
                dot(coarse[...], wide[:, m : m + PART])
                for m in range(0, KERNELS * FREQ, PART)
            ],
            1,
        )
        tot_re = tot_im = None
        for k in range(KERNELS):
            cut = g[:, k * FREQ : (k + 1) * FREQ]
            g_re, g_im = cut[:FREQ], cut[FREQ:]
            h_re, h_im = kern[k, 0], kern[k, 1]
            one_re = h_re * g_re + h_im * g_im
            one_im = h_re * g_im - h_im * g_re
            tot_re = one_re if k == 0 else tot_re + one_re
            tot_im = one_im if k == 0 else tot_im + one_im
        t.tot_re, t.tot_im = tot_re, tot_im

    def finish(t):
        level = cls_ref[t.slot // COLS, t.slot % COLS]
        size = 0.5 * steps_ref[level - 1]
        tot_re = size * t.tot_re
        tot_im = size * t.tot_im
        v = dot(jnp.concatenate([tot_re, tot_im], 1).astype(BF), fine[...]).astype(BF)
        grad = dot(back[...], jnp.concatenate([v[:, :TILE], v[:, TILE:]], 0))
        here = mask[t.slot]
        trans = jnp.tanh(0.5 * here)
        result[t.home] = here - grad * (1.0 - trans * trans)

    class Tile:
        def __init__(self, i, lane):
            self.home, self.lane = i, lane
            self.i = jnp.minimum(i, count - 1)
            self.slot = slot_ref[self.i]
            self.r = pl.multiple_of(self.slot // COLS * TILE, TILE)

    def batch(b, _):
        start = b * LANES
        tiles = [Tile(start + n, n) for n in range(LANES)]
        for t in tiles:
            spectrum(t)
        for t in tiles:
            forward(t, 0)

        @pl.when(b == 0)
        def _():
            keep()
            lax.fori_loop(0, count, lambda i, _: (goal_copy(i).wait(), 0)[1], 0)

        for t in tiles:
            resist(t)
        for t in tiles:
            adjoint(t, 0)
        for n, t in enumerate(tiles):
            finish(t)
            if n == 0:
                out_copy(start).start()
                continue

            @pl.when(start + n < count)
            def _(n=n):
                out_copy(start + n).start()

        return 0

    lax.fori_loop(0, (count + LANES - 1) // LANES, batch, 0)

    lax.fori_loop(0, count, lambda i, _: (out_copy(i).wait(), 0)[1], 0)
    for s in range(SLOTS):

        @pl.when(cls_ref[s // COLS, s % COLS] <= 0)
        def _(s=s):
            keep_copy(s).wait()


def take_step(cls, steps, mask, target, half_spectra, kernels, tabs):
    hbm = pl.BlockSpec(memory_space=pltpu.HBM)
    vmem = pl.BlockSpec(memory_space=pltpu.VMEM)
    smem = pl.BlockSpec(memory_space=pltpu.SMEM)
    dma = pltpu.SemaphoreType.DMA
    here = pltpu.with_memory_space_constraint
    return pl.pallas_call(
        step_kernel,
        out_shape=jax.ShapeDtypeStruct((ROWS_HERE, COLS_HERE), F32),
        in_specs=[smem, smem, hbm, hbm, vmem, vmem] + [vmem] * len(tabs),
        out_specs=hbm,
        scratch_shapes=[
            pltpu.SMEM((SLOTS,), jnp.int32),
            pltpu.VMEM((MOST, TILE, TILE), BF),
            pltpu.VMEM((SLOTS, TILE, TILE), F32),
            pltpu.VMEM((MOST, TILE, TILE), F32),
            pltpu.VMEM((LANES, KERNELS, GRID, 2 * GRID), BF),
            pltpu.VMEM((LANES, GRID, GRID), F32),
            dma((MOST,)),
            dma((SLOTS,)),
            dma((MOST,)),
            dma((SLOTS,)),
        ],
        compiler_params=pltpu.CompilerParams(vmem_limit_bytes=48 * 1024 * 1024),
        cost_estimate=pl.CostEstimate(
            flops=30_000_000_000, bytes_accessed=40_000_000, transcendentals=3_000_000
        ),
    )(
        cls,
        steps,
        here(mask, pltpu.HBM),
        here(target, pltpu.HBM),
        here(half_spectra, pltpu.VMEM),
        here(kernels, pltpu.VMEM),
        *[here(t, pltpu.VMEM) for t in tabs],
    )


CORNERS = ((-1, -1), (-1, 1), (1, -1), (1, 1))
SIDES = ((-1, 0), (1, 0), (0, -1), (0, 1)) + CORNERS
CHUNK = 256
LATER = 8
CHUNKS = ROWS_HERE // CHUNK
HALF = ROWS_HERE // 2


def near_transform(trans, spread):
    pieces = []
    for c in range(COLS):
        first, last = c * TILE - SIDE, (c + 1) * TILE + SIDE
        low, high = max(first, 0), min(last, COLS_HERE)
        pieces.append(dot(trans[:, low:high], spread[low - first : high - first, :]))
    return pieces


def margin_kernel(
    n_rows,
    n_cols,
    mask_hbm,
    spread_hbm,
    edges_hbm,
    mirror_hbm,
    *rest,
):
    later_in, out, later_out, rest = (
        rest[:LATER],
        rest[LATER],
        rest[LATER + 1 : 2 * LATER + 1],
        rest[2 * LATER + 1 :],
    )
    (
        mask,
        spread,
        edges,
        mirror,
        rows_out,
        cols_out,
        corners_out,
        rows_got,
        cols_got,
        corners_got,
        part,
        strip_sem,
        table_sem,
        chunk_sem,
        later_sem,
        send_sem,
        recv_sem,
    ) = rest
    row, col = lax.axis_index("trow"), lax.axis_index("tcol")

    def near(dr, dc):
        return (lax.rem(row + dr + n_rows, n_rows), lax.rem(col + dc + n_cols, n_cols))

    barrier = pltpu.get_barrier_semaphore()
    for dr, dc in SIDES:
        pl.semaphore_signal(
            barrier, inc=1, device_id=near(dr, dc), device_id_type=pl.DeviceIdType.MESH
        )

    def load(r, height, c, width, sem):
        where = (pl.ds(r, height), pl.ds(c, width))
        return pltpu.make_async_copy(mask_hbm.at[where], mask.at[where], sem)

    inner = ROWS_HERE - 2 * APRON
    strips = [
        load(0, APRON, 0, COLS_HERE, strip_sem.at[0]),
        load(ROWS_HERE - APRON, APRON, 0, COLS_HERE, strip_sem.at[1]),
        load(APRON, inner, 0, SIDE, strip_sem.at[2]),
        load(APRON, inner, COLS_HERE - SIDE, SIDE, strip_sem.at[3]),
    ]
    chunks = []
    for n in range(CHUNKS):
        top = max(n * CHUNK, APRON)
        height = min((n + 1) * CHUNK, ROWS_HERE - APRON) - top
        chunks.append(load(top, height, SIDE, COLS_HERE - 2 * SIDE, chunk_sem.at[n]))
    near_table = pltpu.make_async_copy(spread_hbm, spread, table_sem.at[0])
    edge_table = pltpu.make_async_copy(edges_hbm, edges, table_sem.at[1])
    mirror_table = pltpu.make_async_copy(mirror_hbm, mirror, table_sem.at[2])
    laters = [
        pltpu.make_async_copy(later_in[n], later_out[n], later_sem.at[n]) for n in range(LATER)
    ]
    loads = strips[:2] + [near_table] + strips[2:] + chunks[:1] + [edge_table, mirror_table] + chunks[1:]
    for copy in loads:
        copy.start()

    inside_r = [(row > 0).astype(F32), (row < n_rows - 1).astype(F32)]
    inside_c = [(col > 0).astype(F32), (col < n_cols - 1).astype(F32)]

    def packed(band, side):
        half = band.shape[0] // 2
        upper, lower = band[:half], pltpu.roll(band[half:], APRON, 1)
        if side == 1:
            upper, lower = lower, upper
        lane = lax.broadcasted_iota(jnp.int32, (half, SIDE), 1)
        return jnp.where(lane < APRON, upper, lower).astype(BF)

    strips[0].wait()
    strips[1].wait()
    bands = []
    for side in range(2):
        start = side * (ROWS_HERE - APRON)
        band = jnp.tanh(0.5 * mask[start : start + APRON, :]) * inside_r[side]
        bands.append(band.astype(BF))
        for other in range(2):
            begin = other * (COLS_HERE - SIDE)
            cut = band[:, begin : begin + SIDE] * inside_c[other]
            corners_out[2 * side + other] = packed(cut, other)
    near_table.wait()
    lanes = lax.broadcasted_iota(jnp.int32, (2 * APRON, FREQ), 1)
    zero = jnp.zeros((2 * APRON, FREQ), F32)
    for c, piece in enumerate(near_transform(jnp.concatenate(bands, 0), spread)):
        even, odd = piece[:, :FREQ], piece[:, FREQ:]
        low = jnp.where(lanes < FREQ // 2, even, pltpu.roll(odd, FREQ // 2, 1)).astype(BF)
        zero = jnp.where(lanes == c, pltpu.roll(even, FREQ // 2 + c, 1), zero)
        for side in range(2):
            rows_out[side, c] = low[side * APRON : (side + 1) * APRON]
    for side in range(2):
        rows_out[side, COLS] = zero[side * APRON : (side + 1) * APRON].astype(BF)

    sources = [rows_out.at[0], rows_out.at[1], cols_out.at[0], cols_out.at[1]]
    places = [rows_got.at[1], rows_got.at[0], cols_got.at[1], cols_got.at[0]]
    for n in range(len(CORNERS)):
        sources.append(corners_out.at[n])
        places.append(corners_got.at[len(CORNERS) - 1 - n])
    sends = [
        pltpu.make_async_remote_copy(
            src_ref=sources[n],
            dst_ref=places[n],
            send_sem=send_sem.at[n],
            recv_sem=recv_sem.at[n],
            device_id=near(dr, dc),
            device_id_type=pl.DeviceIdType.MESH,
        )
        for n, (dr, dc) in enumerate(SIDES)
    ]
    pl.semaphore_wait(barrier, len(SIDES))
    for send in sends[:2] + sends[4:]:
        send.start()

    strips[2].wait()
    strips[3].wait()
    for side in range(2):
        start = side * (COLS_HERE - SIDE)
        band = jnp.tanh(0.5 * mask[:, start : start + SIDE]) * inside_c[side]
        cols_out[side] = packed(band, side)
    for send in sends[2:4]:
        send.start()
    for copy in laters:
        copy.start()

    for n in range(CHUNKS):
        chunks[n].wait()
        here = slice(n * CHUNK, (n + 1) * CHUNK)
        pieces = near_transform(jnp.tanh(0.5 * mask[here, :]).astype(BF), spread)
        part[0, here] = pieces[0]
        part[1, here] = pieces[-1]
        for c in range(1, COLS - 1):
            out[c, APRON + n * CHUNK : APRON + (n + 1) * CHUNK] = pieces[c].astype(BF)

    edge_table.wait()
    sends[2].wait()
    sends[3].wait()
    for side, c in ((0, 0), (1, COLS - 1)):
        for h in range(2):
            here = slice(h * HALF, (h + 1) * HALF)
            whole = part[side, here] + dot(cols_got[side], edges[side, h])
            out[c, APRON + h * HALF : APRON + (h + 1) * HALF] = whole.astype(BF)
    sends[0].wait()
    sends[1].wait()
    for send in sends[4:]:
        send.wait()
    mirror_table.wait()
    packs = []
    for side in range(2):
        zero = rows_got[side, COLS].astype(F32)
        for c in range(COLS):
            lane = jnp.where(lanes[:APRON] == c, zero, 0.0).astype(BF)
            packs.append(jnp.concatenate([rows_got[side, c], lane], 1))
    whole = dot(jnp.concatenate(packs, 0), mirror[...])
    for side in range(2):
        start = side * (APRON + ROWS_HERE)
        for c in range(COLS):
            first = (side * COLS + c) * APRON
            value = whole[first : first + APRON]
            other = {0: 0, COLS - 1: 1}.get(c)
            if other is not None:
                got = corners_got[2 * side + other]
                corner = [dot(got, edges[other, h]) for h in range(2)]
                value = value + jnp.concatenate(corner, 0)
            out[c, start : start + APRON] = value.astype(BF)
    for copy in laters:
        copy.wait()


def half_transform(mask, spread, edges, mirror, later, n_rows, n_cols):
    vmem = pl.BlockSpec(memory_space=pltpu.VMEM)
    dma = pltpu.SemaphoreType.DMA
    here = pltpu.with_memory_space_constraint
    rows_shape = (2, COLS + 1, APRON, FREQ)
    cols_shape = (2, HALF, SIDE)
    corners_shape = (len(CORNERS), APRON // 2, SIDE)
    return pl.pallas_call(
        functools.partial(margin_kernel, n_rows, n_cols),
        out_shape=[pltpu.VMEM((COLS, ROWS_HERE + 2 * APRON, 2 * FREQ), BF)]
        + [pltpu.VMEM(a.shape, a.dtype) for a in later],
        in_specs=[pl.BlockSpec(memory_space=pltpu.HBM)] * (4 + LATER),
        out_specs=[vmem] * (1 + LATER),
        scratch_shapes=[
            pltpu.VMEM((ROWS_HERE, COLS_HERE), F32),
            pltpu.VMEM((WIDE, 2 * FREQ), BF),
            pltpu.VMEM((2, 2, SIDE, 2 * FREQ), BF),
            pltpu.VMEM((2 * FREQ, 2 * FREQ), BF),
            pltpu.VMEM(rows_shape, BF),
            pltpu.VMEM(cols_shape, BF),
            pltpu.VMEM(corners_shape, BF),
            pltpu.VMEM(rows_shape, BF),
            pltpu.VMEM(cols_shape, BF),
            pltpu.VMEM(corners_shape, BF),
            pltpu.VMEM((2, ROWS_HERE, 2 * FREQ), F32),
            dma((4,)),
            dma((3,)),
            dma((CHUNKS,)),
            dma((LATER,)),
            dma((len(SIDES),)),
            dma((len(SIDES),)),
        ],
        compiler_params=pltpu.CompilerParams(
            collective_id=0, has_side_effects=True, vmem_limit_bytes=40 * 1024 * 1024
        ),
        cost_estimate=pl.CostEstimate(
            flops=2_000_000_000, bytes_accessed=10_000_000, transcendentals=2_000_000
        ),
    )(*[here(a, pltpu.HBM) for a in (mask, spread, edges, mirror, *later)])


def body(mask_level, target, kernels, step_sizes, density_class, work_list):
    spread, edges, mirror, *tabs = [jnp.asarray(t) for t in tables()]
    half_spectra, kernels, *tabs = half_transform(
        mask_level,
        spread,
        edges,
        mirror,
        [kernels, *tabs],
        lax.axis_size("trow"),
        lax.axis_size("tcol"),
    )
    return take_step(density_class, step_sizes, mask_level, target, half_spectra, kernels, tabs)


def solution(mesh):
    return jax.shard_map(
        body,
        mesh=mesh,
        in_specs=(P("trow", "tcol"), P("trow", "tcol"), P(), P(), P("trow", "tcol"), P()),
        out_specs=P("trow", "tcol"),
        check_vma=False,
    )
```

```python
import functools

import jax
import jax.numpy as jnp
import ml_dtypes
import numpy as np
from jax import lax
from jax.experimental import pallas as pl
from jax.experimental.pallas import tpu as pltpu
from jax.sharding import PartitionSpec as P

TILE = 512
APRON = 64
PAD = TILE + 2 * APRON
FREQ = 128
KERNELS = 12
MOST = 4
SLOTS = 8
LANES = 2
PART = 512
COLS = 4
GRID = 256
SIDE = 128
WIDE = TILE + 2 * SIDE
ROWS_HERE = 2 * TILE
COLS_HERE = COLS * TILE
BF = jnp.bfloat16
F32 = jnp.float32


def tables():
    freq = np.arange(FREQ, dtype=np.int64) - FREQ // 2

    def waves(count, period):
        turns = (freq[:, None] * np.arange(count)[None, :]) % period
        angles = turns * (2.0 * np.pi / period)
        return np.cos(angles), np.sin(angles)

    cos, sin = waves(PAD, PAD)
    spread = np.zeros((WIDE, 2 * FREQ))
    spread[SIDE - APRON : SIDE + TILE + APRON] = np.concatenate([cos, sin], 0).T
    ends = [spread[:SIDE], spread[WIDE - SIDE :]]
    edges = np.stack([np.stack([e, np.roll(e, APRON, 0)]) for e in ends])
    rows = np.concatenate([cos, sin], 0)
    half = FREQ // 2
    mirror = np.zeros((2 * FREQ, 2 * FREQ))
    for n in range(half):
        mirror[n, n] = mirror[half + n, FREQ + n] = 1.0
        if n:
            mirror[n, FREQ - n] = 1.0
            mirror[half + n, 2 * FREQ - n] = -1.0
    mirror[FREQ:, half] = 1.0
    cg, sg = waves(GRID, GRID)
    coarse = np.block([[cg, sg], [-sg, cg]])
    core_cos, core_sin = cos[:, APRON : APRON + TILE], sin[:, APRON : APRON + TILE]
    fine = np.block([[core_cos, core_sin], [-core_sin, core_cos]])
    back = np.concatenate([core_cos, -core_sin], 0).T
    gap = np.arange(APRON, APRON + TILE)[:, None] - np.arange(GRID)[None, :] * (PAD / GRID)
    degree = np.arange(1, FREQ)
    lift = 1.0 + 2.0 * np.cos(gap[:, :, None] * degree * (2.0 * np.pi / PAD)).sum(2)
    lift = lift / GRID
    return [
        np.ascontiguousarray(t).astype(ml_dtypes.bfloat16)
        for t in (spread, edges, mirror, rows, coarse, coarse.T, lift, lift.T, fine, back)
    ]


def dot(a, b):
    return jnp.dot(a, b, preferred_element_type=F32)


def step_kernel(
    cls_ref,
    steps_ref,
    mask_hbm,
    target_hbm,
    half_spectra,
    kern,
    rows,
    coarse,
    coarse_t,
    lift,
    lift_t,
    fine,
    back,
    out_hbm,
    slot_ref,
    goal,
    mask,
    result,
    field,
    inten,
    goal_sem,
    mask_sem,
    out_sem,
    keep_sem,
):
    count = jnp.int32(0)
    for s in range(SLOTS):
        busy = cls_ref[s // COLS, s % COLS] > 0

        @pl.when(busy)
        def _(s=s, count=count):
            slot_ref[count] = s

        count = count + busy.astype(jnp.int32)

    def corner(s):
        r, c = s // COLS, s % COLS
        return pl.multiple_of(r * TILE, TILE), pl.multiple_of(c * TILE, TILE)

    def goal_copy(i):
        r, c = corner(slot_ref[i])
        return pltpu.make_async_copy(
            target_hbm.at[pl.ds(r, TILE), pl.ds(c, TILE)], goal.at[i], goal_sem.at[i]
        )

    def mask_copy(s):
        r, c = (s // COLS) * TILE, (s % COLS) * TILE
        return pltpu.make_async_copy(
            mask_hbm.at[pl.ds(r, TILE), pl.ds(c, TILE)], mask.at[s], mask_sem.at[s]
        )

    def keep_copy(s):
        r, c = (s // COLS) * TILE, (s % COLS) * TILE
        return pltpu.make_async_copy(
            mask.at[s], out_hbm.at[pl.ds(r, TILE), pl.ds(c, TILE)], keep_sem.at[s]
        )

    def out_copy(i):
        r, c = corner(slot_ref[i])
        return pltpu.make_async_copy(
            result.at[i], out_hbm.at[pl.ds(r, TILE), pl.ds(c, TILE)], out_sem.at[i]
        )

    def fetch(i, _):
        goal_copy(i).start()
        return 0

    lax.fori_loop(0, count, fetch, 0)
    for s in range(SLOTS):
        mask_copy(s).start()

    def keep():
        for s in range(SLOTS):
            mask_copy(s).wait()

            @pl.when(cls_ref[s // COLS, s % COLS] <= 0)
            def _(s=s):
                keep_copy(s).start()

    @pl.when(count == 0)
    def _():
        keep()

    def spectrum(t):
        blocks = dot(rows[...], half_spectra[t.slot % COLS, pl.ds(t.r, PAD), :])
        re = blocks[:FREQ, :FREQ] - blocks[FREQ:, FREQ:]
        im = -(blocks[:FREQ, FREQ:] + blocks[FREQ:, :FREQ])
        t.spec_re, t.spec_im = re, im

    def kernel_lanes(part):
        return jnp.concatenate([kern[k, part] for k in range(KERNELS)], 1)

    def forward(t, _):
        h_re, h_im = kernel_lanes(0), kernel_lanes(1)
        re = jnp.concatenate([t.spec_re] * KERNELS, 1)
        im = jnp.concatenate([t.spec_im] * KERNELS, 1)
        z_re = (h_re * re - h_im * im).astype(BF)
        z_im = (h_re * im + h_im * re).astype(BF)
        w = dot(coarse_t[...], jnp.concatenate([z_re, z_im], 0)).astype(BF)
        parts = []
        for k in range(KERNELS):
            cut = w[:, k * FREQ : (k + 1) * FREQ]
            parts.append(jnp.concatenate([cut[:GRID], cut[GRID:]], 1))
        f = dot(jnp.concatenate(parts, 0), coarse[...])
        total = None
        for k in range(KERNELS):
            one = f[k * GRID : (k + 1) * GRID]
            field[t.lane, k] = one.astype(BF)
            square = one[:, :GRID] * one[:, :GRID] + one[:, GRID:] * one[:, GRID:]
            total = square if total is None else total + square
        inten[t.lane] = total - 1.0

    def resist(t):
        half = dot(lift[...], (2.0 * inten[t.lane]).astype(BF)).astype(BF)
        bend = jnp.tanh(dot(half, lift_t[...]))
        weight = (1.0 + bend - 2.0 * goal[t.i].astype(F32)) * (1.0 - bend * bend)
        drop = dot(lift_t[...], weight.astype(BF)).astype(BF)
        pull = (2.0 * dot(drop, lift[...])).astype(BF)
        t.pull = jnp.concatenate([pull, pull], 1)

    def adjoint(t, _):
        pulled = jnp.concatenate([field[t.lane, k] * t.pull for k in range(KERNELS)], 0)
        x = jnp.concatenate(
            [
                dot(pulled[m : m + PART], coarse_t[...]).astype(BF)
                for m in range(0, KERNELS * GRID, PART)
            ],
            0,
        )
        wide = jnp.concatenate(
            [
                jnp.concatenate(
                    [
                        x[k * GRID : (k + 1) * GRID, part * FREQ : (part + 1) * FREQ]
                        for k in range(KERNELS)
                    ],
                    1,
                )
                for part in range(2)
            ],
            0,
        )
        g = jnp.concatenate(
            [
                dot(coarse[...], wide[:, m : m + PART])
                for m in range(0, KERNELS * FREQ, PART)
            ],
            1,
        )
        tot_re = tot_im = None
        for k in range(KERNELS):
            cut = g[:, k * FREQ : (k + 1) * FREQ]
            g_re, g_im = cut[:FREQ], cut[FREQ:]
            h_re, h_im = kern[k, 0], kern[k, 1]
            one_re = h_re * g_re + h_im * g_im
            one_im = h_re * g_im - h_im * g_re
            tot_re = one_re if k == 0 else tot_re + one_re
            tot_im = one_im if k == 0 else tot_im + one_im
        t.tot_re, t.tot_im = tot_re, tot_im

    def finish(t):
        level = cls_ref[t.slot // COLS, t.slot % COLS]
        size = 0.5 * steps_ref[level - 1]
        tot_re = size * t.tot_re
        tot_im = size * t.tot_im
        v = dot(jnp.concatenate([tot_re, tot_im], 1).astype(BF), fine[...]).astype(BF)
        grad = dot(back[...], jnp.concatenate([v[:, :TILE], v[:, TILE:]], 0))
        here = mask[t.slot]
        trans = jnp.tanh(0.5 * here)
        result[t.home] = here - grad * (1.0 - trans * trans)

    class Tile:
        def __init__(self, i, lane):
            self.home, self.lane = i, lane
            self.i = jnp.minimum(i, count - 1)
            self.slot = slot_ref[self.i]
            self.r = pl.multiple_of(self.slot // COLS * TILE, TILE)

    def batch(b, _):
        start = b * LANES
        tiles = [Tile(start + n, n) for n in range(LANES)]
        for t in tiles:
            spectrum(t)
        for t in tiles:
            forward(t, 0)

        @pl.when(b == 0)
        def _():
            keep()
            lax.fori_loop(0, count, lambda i, _: (goal_copy(i).wait(), 0)[1], 0)

        for t in tiles:
            resist(t)
        for t in tiles:
            adjoint(t, 0)
        for n, t in enumerate(tiles):
            finish(t)
            if n == 0:
                out_copy(start).start()
                continue

            @pl.when(start + n < count)
            def _(n=n):
                out_copy(start + n).start()

        return 0

    lax.fori_loop(0, (count + LANES - 1) // LANES, batch, 0)

    lax.fori_loop(0, count, lambda i, _: (out_copy(i).wait(), 0)[1], 0)
    for s in range(SLOTS):

        @pl.when(cls_ref[s // COLS, s % COLS] <= 0)
        def _(s=s):
            keep_copy(s).wait()


def take_step(cls, steps, mask, target, half_spectra, kernels, tabs):
    hbm = pl.BlockSpec(memory_space=pltpu.HBM)
    vmem = pl.BlockSpec(memory_space=pltpu.VMEM)
    smem = pl.BlockSpec(memory_space=pltpu.SMEM)
    dma = pltpu.SemaphoreType.DMA
    here = pltpu.with_memory_space_constraint
    return pl.pallas_call(
        step_kernel,
        out_shape=jax.ShapeDtypeStruct((ROWS_HERE, COLS_HERE), F32),
        in_specs=[smem, smem, hbm, hbm, vmem, vmem] + [vmem] * len(tabs),
        out_specs=hbm,
        scratch_shapes=[
            pltpu.SMEM((SLOTS,), jnp.int32),
            pltpu.VMEM((MOST, TILE, TILE), BF),
            pltpu.VMEM((SLOTS, TILE, TILE), F32),
            pltpu.VMEM((MOST, TILE, TILE), F32),
            pltpu.VMEM((LANES, KERNELS, GRID, 2 * GRID), BF),
            pltpu.VMEM((LANES, GRID, GRID), F32),
            dma((MOST,)),
            dma((SLOTS,)),
            dma((MOST,)),
            dma((SLOTS,)),
        ],
        compiler_params=pltpu.CompilerParams(vmem_limit_bytes=48 * 1024 * 1024),
        cost_estimate=pl.CostEstimate(
            flops=30_000_000_000, bytes_accessed=40_000_000, transcendentals=3_000_000
        ),
    )(
        cls,
        steps,
        here(mask, pltpu.HBM),
        here(target, pltpu.HBM),
        here(half_spectra, pltpu.VMEM),
        here(kernels, pltpu.VMEM),
        *[here(t, pltpu.VMEM) for t in tabs],
    )


CORNERS = ((-1, -1), (-1, 1), (1, -1), (1, 1))
SIDES = ((-1, 0), (1, 0), (0, -1), (0, 1)) + CORNERS
CHUNK = 512
LATER = 8
CHUNKS = ROWS_HERE // CHUNK
HALF = ROWS_HERE // 2


def near_transform(trans, spread):
    pieces = []
    for c in range(COLS):
        first, last = c * TILE - SIDE, (c + 1) * TILE + SIDE
        low, high = max(first, 0), min(last, COLS_HERE)
        pieces.append(dot(trans[:, low:high], spread[low - first : high - first, :]))
    return pieces


def margin_kernel(
    n_rows,
    n_cols,
    mask_hbm,
    spread_hbm,
    edges_hbm,
    mirror_hbm,
    *rest,
):
    later_in, out, later_out, rest = (
        rest[:LATER],
        rest[LATER],
        rest[LATER + 1 : 2 * LATER + 1],
        rest[2 * LATER + 1 :],
    )
    (
        mask,
        spread,
        edges,
        mirror,
        rows_out,
        cols_out,
        corners_out,
        rows_got,
        cols_got,
        corners_got,
        part,
        strip_sem,
        table_sem,
        chunk_sem,
        later_sem,
        send_sem,
        recv_sem,
    ) = rest
    row, col = lax.axis_index("trow"), lax.axis_index("tcol")

    def near(dr, dc):
        return (lax.rem(row + dr + n_rows, n_rows), lax.rem(col + dc + n_cols, n_cols))

    barrier = pltpu.get_barrier_semaphore()
    for dr, dc in SIDES:
        pl.semaphore_signal(
            barrier, inc=1, device_id=near(dr, dc), device_id_type=pl.DeviceIdType.MESH
        )

    def load(r, height, c, width, sem):
        where = (pl.ds(r, height), pl.ds(c, width))
        return pltpu.make_async_copy(mask_hbm.at[where], mask.at[where], sem)

    inner = ROWS_HERE - 2 * APRON
    strips = [
        load(0, APRON, 0, COLS_HERE, strip_sem.at[0]),
        load(ROWS_HERE - APRON, APRON, 0, COLS_HERE, strip_sem.at[1]),
        load(APRON, inner, 0, SIDE, strip_sem.at[2]),
        load(APRON, inner, COLS_HERE - SIDE, SIDE, strip_sem.at[3]),
    ]
    chunks = []
    for n in range(CHUNKS):
        top = max(n * CHUNK, APRON)
        height = min((n + 1) * CHUNK, ROWS_HERE - APRON) - top
        chunks.append(load(top, height, SIDE, COLS_HERE - 2 * SIDE, chunk_sem.at[n]))
    near_table = pltpu.make_async_copy(spread_hbm, spread, table_sem.at[0])
    edge_table = pltpu.make_async_copy(edges_hbm, edges, table_sem.at[1])
    mirror_table = pltpu.make_async_copy(mirror_hbm, mirror, table_sem.at[2])
    laters = [
        pltpu.make_async_copy(later_in[n], later_out[n], later_sem.at[n]) for n in range(LATER)
    ]
    loads = strips[:2] + [near_table] + strips[2:] + chunks[:1] + [edge_table, mirror_table] + chunks[1:]
    for copy in loads:
        copy.start()

    inside_r = [(row > 0).astype(F32), (row < n_rows - 1).astype(F32)]
    inside_c = [(col > 0).astype(F32), (col < n_cols - 1).astype(F32)]

    def packed(band, side):
        half = band.shape[0] // 2
        upper, lower = band[:half], pltpu.roll(band[half:], APRON, 1)
        if side == 1:
            upper, lower = lower, upper
        lane = lax.broadcasted_iota(jnp.int32, (half, SIDE), 1)
        return jnp.where(lane < APRON, upper, lower).astype(BF)

    strips[0].wait()
    strips[1].wait()
    bands = []
    for side in range(2):
        start = side * (ROWS_HERE - APRON)
        band = jnp.tanh(0.5 * mask[start : start + APRON, :]) * inside_r[side]
        bands.append(band.astype(BF))
        for other in range(2):
            begin = other * (COLS_HERE - SIDE)
            cut = band[:, begin : begin + SIDE] * inside_c[other]
            corners_out[2 * side + other] = packed(cut, other)
    near_table.wait()
    lanes = lax.broadcasted_iota(jnp.int32, (2 * APRON, FREQ), 1)
    zero = jnp.zeros((2 * APRON, FREQ), F32)
    for c, piece in enumerate(near_transform(jnp.concatenate(bands, 0), spread)):
        even, odd = piece[:, :FREQ], piece[:, FREQ:]
        low = jnp.where(lanes < FREQ // 2, even, pltpu.roll(odd, FREQ // 2, 1)).astype(BF)
        zero = jnp.where(lanes == c, pltpu.roll(even, FREQ // 2 + c, 1), zero)
        for side in range(2):
            rows_out[side, c] = low[side * APRON : (side + 1) * APRON]
    for side in range(2):
        rows_out[side, COLS] = zero[side * APRON : (side + 1) * APRON].astype(BF)

    sources = [rows_out.at[0], rows_out.at[1], cols_out.at[0], cols_out.at[1]]
    places = [rows_got.at[1], rows_got.at[0], cols_got.at[1], cols_got.at[0]]
    for n in range(len(CORNERS)):
        sources.append(corners_out.at[n])
        places.append(corners_got.at[len(CORNERS) - 1 - n])
    sends = [
        pltpu.make_async_remote_copy(
            src_ref=sources[n],
            dst_ref=places[n],
            send_sem=send_sem.at[n],
            recv_sem=recv_sem.at[n],
            device_id=near(dr, dc),
            device_id_type=pl.DeviceIdType.MESH,
        )
        for n, (dr, dc) in enumerate(SIDES)
    ]
    pl.semaphore_wait(barrier, len(SIDES))
    for send in sends[:2] + sends[4:]:
        send.start()

    strips[2].wait()
    strips[3].wait()
    for side in range(2):
        start = side * (COLS_HERE - SIDE)
        band = jnp.tanh(0.5 * mask[:, start : start + SIDE]) * inside_c[side]
        cols_out[side] = packed(band, side)
    for send in sends[2:4]:
        send.start()
    for copy in laters:
        copy.start()

    for n in range(CHUNKS):
        chunks[n].wait()
        here = slice(n * CHUNK, (n + 1) * CHUNK)
        pieces = near_transform(jnp.tanh(0.5 * mask[here, :]).astype(BF), spread)
        part[0, here] = pieces[0]
        part[1, here] = pieces[-1]
        for c in range(1, COLS - 1):
            out[c, APRON + n * CHUNK : APRON + (n + 1) * CHUNK] = pieces[c].astype(BF)

    edge_table.wait()
    sends[2].wait()
    sends[3].wait()
    for side, c in ((0, 0), (1, COLS - 1)):
        for h in range(2):
            here = slice(h * HALF, (h + 1) * HALF)
            whole = part[side, here] + dot(cols_got[side], edges[side, h])
            out[c, APRON + h * HALF : APRON + (h + 1) * HALF] = whole.astype(BF)
    sends[0].wait()
    sends[1].wait()
    for send in sends[4:]:
        send.wait()
    mirror_table.wait()
    packs = []
    for side in range(2):
        zero = rows_got[side, COLS].astype(F32)
        for c in range(COLS):
            lane = jnp.where(lanes[:APRON] == c, zero, 0.0).astype(BF)
            packs.append(jnp.concatenate([rows_got[side, c], lane], 1))
    whole = dot(jnp.concatenate(packs, 0), mirror[...])
    for side in range(2):
        start = side * (APRON + ROWS_HERE)
        for c in range(COLS):
            first = (side * COLS + c) * APRON
            value = whole[first : first + APRON]
            other = {0: 0, COLS - 1: 1}.get(c)
            if other is not None:
                got = corners_got[2 * side + other]
                corner = [dot(got, edges[other, h]) for h in range(2)]
                value = value + jnp.concatenate(corner, 0)
            out[c, start : start + APRON] = value.astype(BF)
    for copy in laters:
        copy.wait()


def half_transform(mask, spread, edges, mirror, later, n_rows, n_cols):
    vmem = pl.BlockSpec(memory_space=pltpu.VMEM)
    dma = pltpu.SemaphoreType.DMA
    here = pltpu.with_memory_space_constraint
    rows_shape = (2, COLS + 1, APRON, FREQ)
    cols_shape = (2, HALF, SIDE)
    corners_shape = (len(CORNERS), APRON // 2, SIDE)
    return pl.pallas_call(
        functools.partial(margin_kernel, n_rows, n_cols),
        out_shape=[pltpu.VMEM((COLS, ROWS_HERE + 2 * APRON, 2 * FREQ), BF)]
        + [pltpu.VMEM(a.shape, a.dtype) for a in later],
        in_specs=[pl.BlockSpec(memory_space=pltpu.HBM)] * (4 + LATER),
        out_specs=[vmem] * (1 + LATER),
        scratch_shapes=[
            pltpu.VMEM((ROWS_HERE, COLS_HERE), F32),
            pltpu.VMEM((WIDE, 2 * FREQ), BF),
            pltpu.VMEM((2, 2, SIDE, 2 * FREQ), BF),
            pltpu.VMEM((2 * FREQ, 2 * FREQ), BF),
            pltpu.VMEM(rows_shape, BF),
            pltpu.VMEM(cols_shape, BF),
            pltpu.VMEM(corners_shape, BF),
            pltpu.VMEM(rows_shape, BF),
            pltpu.VMEM(cols_shape, BF),
            pltpu.VMEM(corners_shape, BF),
            pltpu.VMEM((2, ROWS_HERE, 2 * FREQ), F32),
            dma((4,)),
            dma((3,)),
            dma((CHUNKS,)),
            dma((LATER,)),
            dma((len(SIDES),)),
            dma((len(SIDES),)),
        ],
        compiler_params=pltpu.CompilerParams(
            collective_id=0, has_side_effects=True, vmem_limit_bytes=40 * 1024 * 1024
        ),
        cost_estimate=pl.CostEstimate(
            flops=2_000_000_000, bytes_accessed=10_000_000, transcendentals=2_000_000
        ),
    )(*[here(a, pltpu.HBM) for a in (mask, spread, edges, mirror, *later)])


def body(mask_level, target, kernels, step_sizes, density_class, work_list):
    spread, edges, mirror, *tabs = [jnp.asarray(t) for t in tables()]
    half_spectra, kernels, *tabs = half_transform(
        mask_level,
        spread,
        edges,
        mirror,
        [kernels, *tabs],
        lax.axis_size("trow"),
        lax.axis_size("tcol"),
    )
    return take_step(density_class, step_sizes, mask_level, target, half_spectra, kernels, tabs)


def solution(mesh):
    return jax.shard_map(
        body,
        mesh=mesh,
        in_specs=(P("trow", "tcol"), P("trow", "tcol"), P(), P(), P("trow", "tcol"), P()),
        out_specs=P("trow", "tcol"),
        check_vma=False,
    )
```
